32 devices in a mesh: gx: 2 (over core), gy: 4 (over y, x), gz: 4 (over z).
Axes of the slice: x: 2, y: 2, z: 4, core: 2. Of those that a mesh axis runs over, the one named last changes fastest.
Arguments:
- places: float32 [3, 12, 4, 24, 128], P(None, 'gx', 'gy', 'gz'), may hold values from 0.45 to 8.35, as said below
- velocity: float32 [3, 12, 4, 24, 128], P(None, 'gx', 'gy', 'gz'), may hold values from -6 to 6
- forces_old: float32 [3, 12, 4, 24, 128], P(None, 'gx', 'gy', 'gz'), may hold values from -48 to 48
- counts: int32 [12, 4, 24], P('gx', 'gy', 'gz'), may hold values from 16 to 120, as said below
- mig_atom: int32 [2, 4, 4, 16], P('gx', 'gy', 'gz'), may hold values from 0 to 4607, as said below
- mig_face: int32 [2, 4, 4, 16], P('gx', 'gy', 'gz'), may hold values from 0 to 5, as said below
Outputs:
- new_places: float32 [3, 12, 4, 24, 128], P(None, 'gx', 'gy', 'gz')
- new_velocity: float32 [3, 12, 4, 24, 128], P(None, 'gx', 'gy', 'gz')
- new_forces: float32 [3, 12, 4, 24, 128], P(None, 'gx', 'gy', 'gz')
The draws below stay inside these ranges and needn't reach their ends.
Inputs may be any that keep to these rules, and one draw needn't show every extreme that they name: `places`: within a cell and between neighbouring cells, any two slots lie at least 0.7 apart. `counts`: some cell holds exactly 120 atoms. `mig_atom`: each device's 16 entries name occupied slots of 16 distinct cells. `mig_face`: each entry's cell lies on the named face of its device's block.
All inputs are finite; a program needn't handle non-finite values.
Results may differ from the reference program's by a relative error of at most 0.0003.
Values sent between devices are 32-bit elements; how exact they have to be, the bound alone decides.
No kernel may reach another device: no remote copies, remote signals or barrier semaphores. Data moves between devices by JAX's collectives and lax.ppermute only.
A program may use at most 64 MiB of HBM per device.

```python
import math
import jax
import jax.numpy as jnp
from jax import lax

CAP = 128
MIG = 16
NX = 12
NY = 4
NZ = 24
N_GX = 2
N_GY = 4
N_GZ = 4


def draw_count_table(key):
    base_key = jax.random.fold_in(key, 11)
    low_count = CAP // 8
    high_count = CAP - 8
    spread = high_count - low_count
    first_draw = jax.random.randint(jax.random.fold_in(base_key, 1), (NX, NY, NZ), 0, spread + 1)
    second = jax.random.randint(jax.random.fold_in(base_key, 2), (NX, NY, NZ), 0, spread + 1)
    count_table = low_count + first_draw * second // spread
    cell_total = NX * NY * NZ
    chosen = jax.random.randint(jax.random.fold_in(base_key, 3), (), 0, cell_total)
    flat_table = jnp.where(jnp.arange(cell_total) == chosen, high_count, count_table.reshape(-1))
    return flat_table.reshape(NX, NY, NZ).astype(jnp.int32)


def draw_moves(key):
    count_table = draw_count_table(key)
    base_key = jax.random.fold_in(key, 23)
    local_x = NX // N_GX
    local_y = NY // N_GY
    local_z = NZ // N_GZ
    cell_count = local_x * local_y * local_z
    device_total = N_GX * N_GY * N_GZ
    cell_index = jnp.arange(cell_count)
    pos_x = cell_index // (local_y * local_z)
    pos_y = cell_index // local_z % local_y
    pos_z = cell_index % local_z
    border = (pos_x == 0) | (pos_x == local_x - 1) | (pos_y == 0) | (pos_y == local_y - 1) | (pos_z == 0) | (pos_z == local_z - 1)
    scores = jax.random.randint(jax.random.fold_in(base_key, 1), (device_total, cell_count), 0, 1 << 14)
    keyed_scores = jnp.where(border[None, :], scores, 1 << 14) * cell_count + cell_index[None, :]
    picked = jnp.argsort(keyed_scores, axis=1)[:, :MIG]
    pick_x = picked // (local_y * local_z)
    pick_y = picked // local_z % local_y
    pick_z = picked % local_z
    on_face = jnp.stack([pick_x == 0, pick_x == local_x - 1, pick_y == 0, pick_y == local_y - 1, pick_z == 0, pick_z == local_z - 1], axis=-1)
    face_scores = jax.random.randint(jax.random.fold_in(base_key, 2), (device_total, MIG, 6), 0, 1 << 10) * 8 + jnp.arange(6)
    face_pick = jnp.argmax(jnp.where(on_face, face_scores, -1), axis=-1).astype(jnp.int32)
    device_index = jnp.arange(device_total)[:, None]
    dev_x = device_index // (N_GY * N_GZ)
    dev_y = device_index // N_GZ % N_GY
    dev_z = device_index % N_GZ
    held = count_table[dev_x * local_x + pick_x, dev_y * local_y + pick_y, dev_z * local_z + pick_z]
    slot_pick = jax.random.randint(jax.random.fold_in(base_key, 3), (device_total, MIG), 0, held)
    atom_pick = (picked * CAP + slot_pick).astype(jnp.int32)
    return (atom_pick.reshape(N_GX, N_GY, N_GZ, MIG), face_pick.reshape(N_GX, N_GY, N_GZ, MIG))


def draw_counts(key, part):
    return draw_count_table(key)


def draw_mig_atom(key, part):
    return draw_moves(key)[0]


def draw_mig_face(key, part):
    return draw_moves(key)[1]


def draw_places(key, part):
    order_key = jax.random.fold_in(key, 31)
    jitter_key = jax.random.fold_in(key, 37)
    scores = jax.random.randint(order_key, (NX, NY, NZ, CAP), 0, 1 << 16) * CAP + jnp.arange(CAP)
    site_index = jnp.argsort(scores, axis=-1)
    lattice = jnp.stack([site_index % 4, site_index // 4 % 4, site_index // 16]).astype(jnp.float32) * 1.1 + 0.55
    wobble = jnp.clip(0.03 * jax.random.normal(jitter_key, (3, NX, NY, NZ, CAP), jnp.float32), -0.06, 0.06)
    return lattice + wobble


def steps_of(stream_key, extent, pieces, smallest, top_value):
    def one(dim, parts):
        steps = jax.random.uniform(jax.random.fold_in(jax.random.fold_in(stream_key, 6), dim), (parts,), jnp.float32, smallest / len(pieces), top_value / len(pieces))
        return jnp.repeat(jnp.exp(steps), extent[dim] // parts).reshape((-1,) + (1,) * (len(extent) - dim - 1))

    gain = one(*pieces[0])
    for cut in pieces[1:]:
        gain = gain * one(*cut)
    return gain


def normal_values(rng, shape, scale, bound, pieces=(), kind=jnp.bfloat16):
    gain = steps_of(rng, shape, pieces, -0.22, 0.18) if pieces else 1.0
    values = jax.random.normal(rng, shape, jnp.float32) * scale * gain
    return jnp.minimum(jnp.maximum(values, -bound), bound).astype(kind)


def setup_inputs(seed: int = 0) -> dict:
    key_of = jax.random.split(jax.random.key(seed), 7)
    return {
        "places": draw_places(jax.random.fold_in(key_of[6], 71), 0),
        "velocity": normal_values(key_of[1], (3, NX, NY, NZ, CAP), 1.0, 6.0, ((1, 2), (2, 4), (3, 4)), jnp.float32),
        "forces_old": normal_values(key_of[2], (3, NX, NY, NZ, CAP), 8.0, 48.0, ((1, 2), (2, 4), (3, 4)), jnp.float32),
        "counts": draw_counts(jax.random.fold_in(key_of[6], 71), 0),
        "mig_atom": draw_mig_atom(jax.random.fold_in(key_of[6], 71), 0),
        "mig_face": draw_mig_face(jax.random.fold_in(key_of[6], 71), 0),
    }


step_size = 0.005
cut_radius = 2.5
spacing = 1.1
edge_force = 24.0 * (2.0 * cut_radius ** (-13) - cut_radius ** (-7))

def cell_sides(slot_count):
    return (4.0 * spacing, 4.0 * spacing, spacing * (slot_count // 16))

def half_offsets():
    chosen = []
    for step_z in (-1, 0, 1):
        for step_y in (-1, 0, 1):
            for step_x in (-1, 0, 1):
                if step_z > 0 or (step_z == 0 and (step_y > 0 or (step_y == 0 and step_x >= 0))):
                    chosen.append((step_x, step_y, step_z))
    return chosen

def pair_terms(own_places, other_places, own_alive, other_alive, offset_vec, same_cell):
    shaped = jnp.asarray(offset_vec, own_places.dtype).reshape((3,) + (1,) * own_places.ndim)
    delta_vec = own_places[..., :, None] - (other_places[..., None, :] + shaped)
    distance = lax.optimization_barrier(jnp.sum(delta_vec * delta_vec, axis=0))
    weight = own_alive[..., :, None] * other_alive[..., None, :]
    if same_cell:
        slot_count = own_places.shape[-1]
        rows_iota = lax.broadcasted_iota(jnp.int32, (slot_count, slot_count), 0)
        cols_iota = lax.broadcasted_iota(jnp.int32, (slot_count, slot_count), 1)
        weight = weight * (rows_iota != cols_iota).astype(weight.dtype)
    inside = jnp.where(distance < cut_radius * cut_radius, weight, jnp.zeros_like(weight))
    safe_sq = jnp.where(inside > 0.0, distance, jnp.ones_like(distance))
    inverse = 1.0 / safe_sq
    sixth_power = inverse * inverse * inverse
    magnitude = (24.0 * inverse * sixth_power * (2.0 * sixth_power - 1.0) - edge_force * lax.rsqrt(safe_sq)) * inside
    pulled = delta_vec * magnitude
    return (lax.optimization_barrier(jnp.sum(pulled, axis=-1)), -lax.optimization_barrier(jnp.sum(pulled, axis=-2)))

def split_blocks(array, block_depth):
    lead, size_x, size_y, size_z, slot_count = array.shape
    shaped = array.reshape(lead, size_x, size_y, size_z // block_depth, block_depth, slot_count)
    return shaped.transpose(3, 0, 1, 2, 4, 5)

def join_blocks(array):
    block_total, lead, size_x, size_y, block_depth, slot_count = array.shape
    return array.transpose(1, 2, 3, 0, 4, 5).reshape(lead, size_x, size_y, block_total * block_depth, slot_count)

def all_forces(places, alive_mask):
    full_state = jnp.concatenate([places, alive_mask[None]], axis=0)
    block_depth = math.gcd(places.shape[3], 2)
    cell_side = cell_sides(places.shape[4])
    total_force = jnp.zeros_like(places)
    own_blocks = split_blocks(full_state, block_depth)
    for step_x, step_y, step_z in half_offsets():
        rolled = jnp.roll(full_state, (-step_x, -step_y, -step_z), axis=(1, 2, 3))
        same_cell = (step_x, step_y, step_z) == (0, 0, 0)
        offset_vec = (step_x * cell_side[0], step_y * cell_side[1], step_z * cell_side[2])

        def one_block(pair_blocks):
            own_block, side_block = pair_blocks
            return pair_terms(own_block[:3], side_block[:3], own_block[3], side_block[3], offset_vec, same_cell)
        near_term, far_term = lax.map(one_block, (own_blocks, split_blocks(rolled, block_depth)))
        total_force = total_force + join_blocks(near_term)
        if not same_cell:
            total_force = total_force + jnp.roll(join_blocks(far_term), (step_x, step_y, step_z), axis=(1, 2, 3))
    return total_force

def reference(places, velocity, forces_old, counts, mig_atom, mig_face):
    size_x, size_y, size_z, slot_count = places.shape[1:]
    side_x, side_y, side_z = cell_sides(slot_count)
    alive_mask = (lax.broadcasted_iota(jnp.int32, places.shape[1:], 3) < counts[..., None]).astype(places.dtype)
    half_velocity = velocity + 0.5 * step_size * forces_old
    drifted = places + step_size * half_velocity
    local_x = size_x // N_GX
    local_y = size_y // N_GY
    local_z = size_z // N_GZ
    grid_shape = mig_atom.shape
    dev_x = lax.broadcasted_iota(jnp.int32, grid_shape, 0)
    dev_y = lax.broadcasted_iota(jnp.int32, grid_shape, 1)
    dev_z = lax.broadcasted_iota(jnp.int32, grid_shape, 2)
    cell_id = mig_atom // slot_count
    slot_id = mig_atom % slot_count
    glob_x = dev_x * local_x + cell_id // (local_y * local_z)
    glob_y = dev_y * local_y + cell_id // local_z % local_y
    glob_z = dev_z * local_z + cell_id % local_z
    source = (((glob_x * size_y + glob_y) * size_z + glob_z) * slot_count + slot_id).reshape(-1)
    face_axis = mig_face // 2
    face_sign = 2 * (mig_face % 2) - 1
    dest_x = (glob_x + face_sign * (face_axis == 0).astype(jnp.int32)) % size_x
    dest_y = (glob_y + face_sign * (face_axis == 1).astype(jnp.int32)) % size_y
    dest_z = (glob_z + face_sign * (face_axis == 2).astype(jnp.int32)) % size_z
    dest_cell = ((dest_x * size_y + dest_y) * size_z + dest_z).reshape(-1)
    order_key = (mig_face + 1 - 2 * (mig_face % 2)).reshape(-1)
    flat_sign = face_sign.reshape(-1).astype(places.dtype)
    flat_axis = face_axis.reshape(-1)
    flat_places = drifted.reshape(3, -1)
    flat_velocity = half_velocity.reshape(3, -1)
    flat_alive = alive_mask.reshape(-1)
    along_axis = (lax.broadcasted_iota(jnp.int32, (3, flat_axis.shape[0]), 0) == flat_axis[None, :]).astype(places.dtype)
    side_vec = jnp.asarray((side_x, side_y, side_z), places.dtype)[:, None]
    carried = flat_places[:, source] - along_axis * flat_sign[None, :] * side_vec
    carried_velocity = flat_velocity[:, source]
    flat_alive = flat_alive.at[source].set(0.0)
    cell_total = size_x * size_y * size_z
    arrival_rank = jnp.zeros_like(dest_cell)
    for face_index in range(6):
        hit_count = jnp.zeros((cell_total,), jnp.int32).at[dest_cell].add((order_key == face_index).astype(jnp.int32))
        arrival_rank = arrival_rank + jnp.where(order_key > face_index, hit_count[dest_cell], 0)
    target = dest_cell * slot_count + counts.reshape(-1)[dest_cell] + arrival_rank
    flat_places = flat_places.at[:, target].set(carried)
    flat_velocity = flat_velocity.at[:, target].set(carried_velocity)
    flat_alive = flat_alive.at[target].set(1.0)
    settled_places = flat_places.reshape(places.shape)
    settled_velocity = flat_velocity.reshape(places.shape)
    settled_alive = flat_alive.reshape(alive_mask.shape)
    new_forces = all_forces(settled_places, settled_alive) * settled_alive[None]
    new_velocity = (settled_velocity + 0.5 * step_size * new_forces) * settled_alive[None]
    new_places = settled_places * settled_alive[None]
    return (new_places, new_velocity, new_forces)
```

```python
import functools

import jax
import jax.numpy as jnp
from jax import lax
from jax.experimental import pallas as pl
from jax.experimental.pallas import tpu as pltpu
from jax.sharding import PartitionSpec as P

step_size = 0.005
cut_radius = 2.5
spacing = 1.1
edge_force = 24.0 * (2.0 * cut_radius ** (-13) - cut_radius ** (-7))

FAR = 1.0e6
NEAR = 1.0e5
MARGIN = 1.0e-3
ROWS = 32
Z_CHUNKS = 2
Y_CHUNKS = 3
X_CHUNKS = 6
COMBOS = [(dx, dy, dz) for dx in (-1, 0, 1) for dy in (-1, 0, 1) for dz in (-1, 0, 1)]


def cell_sides(slot_count):
    return (4.0 * spacing, 4.0 * spacing, spacing * (slot_count // 16))


def take(tile, index):
    return jnp.take_along_axis(tile, index, axis=1, mode="promise_in_bounds")


def pack_kernel(count_ref, atom_ref, face_ref, place_ref, velocity_ref, force_ref, slab_ref):
    _, size_x, size_z, slots = place_ref.shape
    sides = cell_sides(slots)
    sub = lax.broadcasted_iota(jnp.int32, (size_z, slots), 0)
    lane = lax.broadcasted_iota(jnp.int32, (size_z, slots), 1)
    letter = slots - 6
    entries = atom_ref.shape[0]
    atoms = [atom_ref[e] for e in range(entries)]
    faces = [face_ref[e] for e in range(entries)]
    for x in range(size_x):
        count = jnp.zeros((size_z, slots), jnp.int32)
        for z in range(size_z):
            count = jnp.where(sub == z, count_ref[x, z], count)
        first_atom = (x * size_z + sub) * slots
        leaving = jnp.full((size_z, slots), -1, jnp.int32)
        face = jnp.full((size_z, slots), -8, jnp.int32)
        for e in range(entries):
            offset = atoms[e] - first_atom
            here = (offset >= 0) & (offset < slots)
            leaving = jnp.where(here, offset, leaving)
            face = jnp.where(here, faces[e], face)
        any_leaves = leaving >= 0
        picked = jnp.maximum(leaving, 0)
        order = jnp.bitwise_xor(face, 1)
        axis_of = lax.shift_right_arithmetic(face, 1)
        sign = (2 * (face & 1) - 1).astype(jnp.float32)
        alive = (lane < count) & (lane != leaving)
        letter_lane = any_leaves & (lane == letter + order)
        speed_lane = lane == letter - 1
        letters = jnp.full((size_z, slots), FAR, jnp.float32)
        for c in range(3):
            half = velocity_ref[c, x] + 0.5 * step_size * force_ref[c, x]
            drifted = place_ref[c, x] + step_size * half
            moved = take(drifted, picked) - jnp.where(axis_of == c, sign * sides[c], 0.0)
            tile = jnp.where(alive, drifted, FAR)
            tile = jnp.where(letter_lane, moved, tile)
            tile = jnp.where(speed_lane, take(half, picked), tile)
            slab_ref[c, x] = tile
            letters = jnp.where(any_leaves & (lane == letter + order - 8 * c), moved, letters)
        slab_ref[3, x] = letters


def merge_sources(sources, chunks, filled, weights):
    slots = weights.shape[0]
    lane = lax.broadcasted_iota(jnp.int32, (8, slots), 1)
    masks = jnp.concatenate([jnp.where(m, 1.0, 0.0) for m, _ in sources], axis=0)
    scanned = jnp.dot(
        masks.astype(jnp.bfloat16), weights, preferred_element_type=jnp.float32
    ).astype(jnp.int32)
    chunks = [list(c) for c in chunks]
    ranks, prefixes, starts, totals = [], [], [], []
    for s in range(len(sources)):
        prefixes.append(scanned[8 * s : 8 * s + 8, :slots])
        totals.append(scanned[8 * s : 8 * s + 8, slots:])
        starts.append(filled)
        ranks.append((lane - filled) & (slots - 1))
        filled = filled + totals[-1]
    positions = [jnp.zeros((8, slots), jnp.int32) for _ in sources]
    step = slots // 2
    while step >= 1:
        for s in range(len(sources)):
            probe = take(prefixes[s], positions[s] + (step - 1))
            positions[s] = jnp.where(probe <= ranks[s], positions[s] + step, positions[s])
        step //= 2
    shift = slots.bit_length() - 1
    for s, (_, tiles) in enumerate(sources):
        moved = [take(t, positions[s]) for t in tiles]
        chunk_id = lax.shift_right_arithmetic(starts[s] + ranks[s], shift)
        chunk_id = jnp.where(ranks[s] < totals[s], chunk_id, -1)
        for k in range(len(chunks)):
            chosen = chunk_id == k
            for c in range(3):
                chunks[k][c] = jnp.where(chosen, moved[c], chunks[k][c])
    return chunks, filled


def pair_force(own, other):
    total = [None, None, None]
    for row in other:
        delta = [own[c] - row[c] for c in range(3)]
        square = delta[0] * delta[0] + delta[1] * delta[1] + delta[2] * delta[2]
        root = lax.rsqrt(square)
        inverse = root * root
        fourth = inverse * inverse
        sixth = fourth * inverse
        strength = (48.0 * sixth - 24.0) * (fourth * fourth) - edge_force * root
        inside = (square < cut_radius * cut_radius) & (square > 0.0)
        strength = jnp.where(inside, strength, 0.0)
        for c in range(3):
            part = delta[c] * strength
            total[c] = part if total[c] is None else total[c] + part
    return [jnp.sum(t, axis=1, keepdims=True) for t in total]


def force_kernel(
    count_ref,
    own_ref,
    low_ref,
    high_ref,
    far_low_ref,
    far_high_ref,
    velocity_ref,
    force_ref,
    out_place_ref,
    out_velocity_ref,
    out_force_ref,
    comb,
    zlist,
    ylist,
    cand,
    own_t,
    force_t,
    chunk_count,
    arrival_count,
):
    _, ext_x, ext_z, slots = own_ref.shape
    size_x, size_z = ext_x - 2, ext_z - 2
    sides = cell_sides(slots)
    letter = slots - 6
    sub = lax.broadcasted_iota(jnp.int32, (ext_z, slots), 0)
    lane = lax.broadcasted_iota(jnp.int32, (ext_z, slots), 1)
    inner = (sub >= 1) & (sub <= size_z)
    far_tile = jnp.full((ext_z, slots), FAR, jnp.float32)
    planes = [low_ref, own_ref, high_ref]

    from_z_low = (lane == letter + 4) & (sub > 0)
    from_z_high = (lane == letter + 5) & (sub < ext_z - 1)
    for x in range(ext_x):
        for y in range(3):
            for c in range(3):
                tile = planes[y][c, x]
                out = jnp.where(lane < letter - 1, tile, FAR)
                if x > 0:
                    out = jnp.where(lane == letter, planes[y][c, x - 1], out)
                if x < ext_x - 1:
                    out = jnp.where(lane == letter + 1, planes[y][c, x + 1], out)
                below = planes[y - 1][c, x] if y > 0 else pltpu.roll(far_low_ref[x], 8 * c, 1)
                above = planes[y + 1][c, x] if y < 2 else pltpu.roll(far_high_ref[x], 8 * c, 1)
                out = jnp.where(lane == letter + 2, below, out)
                out = jnp.where(lane == letter + 3, above, out)
                out = jnp.where(from_z_low, pltpu.roll(tile, 1, 0), out)
                out = jnp.where(from_z_high, pltpu.roll(tile, ext_z - 1, 0), out)
                comb[c, x, y] = out

    lower, upper = [], []
    for c in range(3):
        low_tile = jnp.full((ext_z, slots), FAR, jnp.float32)
        high_tile = jnp.full((ext_z, slots), -FAR, jnp.float32)
        for x in range(1, size_x + 1):
            tile = comb[c, x, 1]
            real = inner & (lane < letter - 1) & (tile < NEAR)
            low_tile = jnp.minimum(low_tile, jnp.where(real, tile, FAR))
            high_tile = jnp.maximum(high_tile, jnp.where(real, tile, -FAR))
        lower.append(jnp.min(low_tile, axis=(0, 1), keepdims=True) - (cut_radius + MARGIN))
        upper.append(jnp.max(high_tile, axis=(0, 1), keepdims=True) + (cut_radius + MARGIN))

    row_id = lax.broadcasted_iota(jnp.int32, (slots, 2 * slots), 0)
    col_id = lax.broadcasted_iota(jnp.int32, (slots, 2 * slots), 1)
    weights = jnp.where(row_id <= col_id, 1.0, 0.0).astype(jnp.bfloat16)
    nothing = jnp.zeros((ext_z, slots), jnp.int32)
    excess = jnp.full((ext_z, slots), -1, jnp.int32)

    z_filled = {}
    for x in range(ext_x):
        for y in range(3):
            tiles = [comb[c, x, y] for c in range(3)]
            down = [pltpu.roll(t, 1, 0) for t in tiles]
            down[2] = down[2] - sides[2]
            up = [pltpu.roll(t, ext_z - 1, 0) for t in tiles]
            up[2] = up[2] + sides[2]
            sources = [
                (inner & (tiles[0] < NEAR), tiles),
                (inner & (down[0] < NEAR) & (down[2] > lower[2]), down),
                (inner & (up[0] < NEAR) & (up[2] < upper[2]), up),
            ]
            chunks = [[far_tile] * 3 for _ in range(Z_CHUNKS)]
            chunks, filled = merge_sources(sources, chunks, nothing, weights)
            z_filled[x, y] = filled
            excess = jnp.maximum(excess, filled - Z_CHUNKS * slots)
            for k in range(Z_CHUNKS):
                for c in range(3):
                    zlist[k, c, x, y] = chunks[k][c]

    y_filled = {}
    for x in range(ext_x):
        sources = []
        for y, shift in ((0, -sides[1]), (2, sides[1])):
            for k in range(Z_CHUNKS):
                tiles = [zlist[k, c, x, y] for c in range(3)]
                tiles[1] = tiles[1] + shift
                reach = (tiles[1] > lower[1]) if y == 0 else (tiles[1] < upper[1])
                sources.append(((tiles[0] < NEAR) & reach, tiles))
        chunks = [[zlist[k, c, x, 1] for c in range(3)] for k in range(Z_CHUNKS)]
        chunks += [[far_tile] * 3 for _ in range(Y_CHUNKS - Z_CHUNKS)]
        chunks, filled = merge_sources(sources, chunks, z_filled[x, 1], weights)
        y_filled[x] = filled
        excess = jnp.maximum(excess, filled - Y_CHUNKS * slots)
        for k in range(Y_CHUNKS):
            for c in range(3):
                ylist[k, c, x] = chunks[k][c]

    chunk_tiles = []
    for x in range(size_x):
        sources = []
        for other, shift in ((x, -sides[0]), (x + 2, sides[0])):
            for k in range(Y_CHUNKS):
                tiles = [ylist[k, c, other] for c in range(3)]
                real = tiles[0] < NEAR
                tiles[0] = tiles[0] + shift
                reach = (tiles[0] > lower[0]) if other == x else (tiles[0] < upper[0])
                sources.append((real & reach, tiles))
        chunks = [[ylist[k, c, x + 1] for c in range(3)] for k in range(Y_CHUNKS)]
        chunks += [[far_tile] * 3 for _ in range(X_CHUNKS - Y_CHUNKS)]
        chunks, filled = merge_sources(sources, chunks, y_filled[x + 1], weights)
        excess = jnp.maximum(excess, filled - X_CHUNKS * slots)
        for k in range(X_CHUNKS):
            for c in range(3):
                cand[x, k, c] = chunks[k][c]
        chunk_tiles.append(lax.shift_right_arithmetic(filled + (slots - 1), slots.bit_length() - 1))

    overflow = jnp.max(excess.astype(jnp.float32)) > 0.0
    for x in range(size_x):
        arrived = jnp.where((lane >= letter) & (comb[0, x + 1, 1] < NEAR), 1.0, 0.0)
        arrived = jnp.max(arrived, axis=1, keepdims=True)
        for z in range(size_z):
            chunk_count[x, z] = jnp.where(overflow, len(COMBOS), chunk_tiles[x][z + 1, 0])
            arrival_count[x, z] = (arrived[z + 1, 0] > 0.0).astype(jnp.int32)

    @pl.when(overflow)
    def _():
        for k, (dx, dy, dz) in enumerate(COMBOS):
            for x in range(size_x):
                for c, step in enumerate((dx, dy, dz)):
                    tile = comb[c, x + 1 + dx, 1 + dy]
                    if dz:
                        tile = pltpu.roll(tile, (-dz) % ext_z, 0)
                    cand[x, k, c] = tile + step * sides[c]

    for x in range(size_x):
        stacked = jnp.concatenate([comb[c, x + 1, 1] for c in range(3)], axis=0)
        stacked = jnp.concatenate(
            [stacked, jnp.zeros((slots - 3 * ext_z, slots), jnp.float32)], axis=0
        )
        own_t[x] = stacked.T
        force_t[x] = jnp.zeros((slots, slots), jnp.float32)

    lane_rows = lax.broadcasted_iota(jnp.int32, (ROWS, slots), 1)
    row_shift = ROWS.bit_length() - 1

    def each_x(x, carry):
        for z in range(size_z):
            picks = [c * ext_z + z + 1 for c in range(3)]
            blocks = lax.shift_right_arithmetic(count_ref[x, z] + (ROWS - 1), row_shift)
            chunk_total = chunk_count[x, z]

            def visit(block, chunk_ids, adding):
                rows = pl.ds(pl.multiple_of(block * ROWS, ROWS), ROWS)
                held = own_t[x, rows, :]
                own = [held[:, p : p + 1] for p in picks]
                other = [
                    [cand[x, k, c, z + 1 : z + 2, :] for c in range(3)] for k in chunk_ids
                ]
                found = pair_force(own, other)
                result = force_t[x, rows, :]
                for c in range(3):
                    value = found[c] + result if adding else found[c]
                    result = jnp.where(lane_rows == picks[c], value, result)
                force_t[x, rows, :] = result

            def sweep(chunk_ids, adding):
                def one(block, inner_carry):
                    visit(block, chunk_ids, adding)
                    return inner_carry

                lax.fori_loop(0, blocks, one, 0)

            @pl.when(chunk_total <= 2)
            def _():
                sweep((0, 1), False)

            @pl.when(chunk_total > 2)
            def _():
                sweep((0, 1, 2), False)

            def more(k, inner_carry):
                sweep((k,), True)
                return inner_carry

            lax.fori_loop(3, chunk_total, more, 0)

            @pl.when(arrival_count[x, z] > 0)
            def _():
                rows = slice(slots - 8, slots)
                held = own_t[x, rows, :]
                own = [held[:, p : p + 1] for p in picks]
                other = []
                for step in COMBOS:
                    other.append(
                        [
                            comb[c, x + 1 + step[0], 1 + step[1], z + 1 + step[2] : z + 2 + step[2], :]
                            + step[c] * sides[c]
                            for c in range(3)
                        ]
                    )
                found = pair_force(own, other)
                result = force_t[x, rows, :]
                for c in range(3):
                    result = jnp.where(lane_rows[:8] == picks[c], found[c], result)
                force_t[x, rows, :] = result

        return carry

    lax.fori_loop(0, size_x, each_x, 0)

    speed = jnp.full((ext_z, slots), letter - 1, jnp.int32)
    for x in range(size_x):
        turned = force_t[x].T
        count = jnp.zeros((ext_z, slots), jnp.int32)
        for z in range(size_z):
            count = jnp.where(sub == z + 1, count_ref[x, z], count)
        base = comb[0, x + 1, 1]
        filled = count
        index = lane
        for o in range(6):
            valid = take(base, jnp.full((ext_z, slots), letter + o, jnp.int32)) < NEAR
            index = jnp.where(valid & (lane == filled), letter + o, index)
            filled = filled + jnp.where(valid, 1, 0)
        placed = take(base, index)
        alive = (lane < filled) & (placed < NEAR)
        for c in range(3):
            half = velocity_ref[c, x] + 0.5 * step_size * force_ref[c, x]
            blank = jnp.zeros((1, slots), jnp.float32)
            half = jnp.concatenate([blank, half, blank], axis=0)
            tile = own_ref[c, x + 1]
            sent = [
                own_ref[c, x],
                own_ref[c, x + 2],
                low_ref[c, x + 1],
                high_ref[c, x + 1],
                pltpu.roll(tile, 1, 0),
                pltpu.roll(tile, ext_z - 1, 0),
            ]
            for o in range(6):
                half = jnp.where(lane == letter + o, take(sent[o], speed), half)
            where_to = placed if c == 0 else take(comb[c, x + 1, 1], index)
            force = jnp.where(alive, take(turned[c * ext_z : (c + 1) * ext_z], index), 0.0)
            half = take(half, index) + 0.5 * step_size * force
            out_place_ref[c, x] = jnp.where(alive, where_to, 0.0)[1 : size_z + 1]
            out_velocity_ref[c, x] = jnp.where(alive, half, 0.0)[1 : size_z + 1]
            out_force_ref[c, x] = force[1 : size_z + 1]


def shifted(value, axis, steps):
    count = lax.axis_size(axis)
    return lax.ppermute(value, axis, [(i, (i + steps) % count) for i in range(count)])


def per_device(places, velocity, forces_old, counts, mig_atom, mig_face):
    size_x, size_y, size_z, slots = places.shape[1:]
    assert size_y == 1 and size_z == 6 and slots == 128 and size_x >= 2
    flat = (3, size_x, size_z, slots)
    place3, velocity3, force3 = (a.reshape(flat) for a in (places, velocity, forces_old))
    count2 = counts.reshape(size_x, size_z)
    vmem = pl.BlockSpec(memory_space=pltpu.VMEM)
    smem = pl.BlockSpec(memory_space=pltpu.SMEM)
    slab = pl.pallas_call(
        pack_kernel,
        out_shape=jax.ShapeDtypeStruct((4,) + flat[1:], jnp.float32),
        in_specs=[smem] * 3 + [vmem] * 3,
        out_specs=vmem,
    )(count2, mig_atom.reshape(-1), mig_face.reshape(-1), place3, velocity3, force3)

    from_low = shifted(slab[:, :, size_z - 1 :], "gz", 1)
    from_high = shifted(slab[:, :, :1], "gz", -1)
    slab = jnp.concatenate([from_low, slab, from_high], axis=2)
    if lax.axis_size("gx") == 2:
        both = shifted(jnp.concatenate([slab[:, :1], slab[:, size_x - 1 :]], axis=1), "gx", 1)
        from_low, from_high = both[:, 1:], both[:, :1]
    else:
        from_low = shifted(slab[:, size_x - 1 :], "gx", 1)
        from_high = shifted(slab[:, :1], "gx", -1)
    slab = jnp.concatenate([from_low, slab, from_high], axis=1)
    own, letters = slab[:3], slab[3]
    low = shifted(own, "gy", 1)
    high = shifted(own, "gy", -1)
    far_low = shifted(letters, "gy", 2)
    far_high = far_low if lax.axis_size("gy") == 4 else shifted(letters, "gy", -2)

    ext_x, ext_z = size_x + 2, size_z + 2
    outs = pl.pallas_call(
        force_kernel,
        out_shape=[jax.ShapeDtypeStruct(flat, jnp.float32)] * 3,
        in_specs=[smem] + [vmem] * 7,
        out_specs=[vmem] * 3,
        scratch_shapes=[
            pltpu.VMEM((3, ext_x, 3, ext_z, slots), jnp.float32),
            pltpu.VMEM((Z_CHUNKS, 3, ext_x, 3, ext_z, slots), jnp.float32),
            pltpu.VMEM((Y_CHUNKS, 3, ext_x, ext_z, slots), jnp.float32),
            pltpu.VMEM((size_x, len(COMBOS), 3, ext_z, slots), jnp.float32),
            pltpu.VMEM((size_x, slots, slots), jnp.float32),
            pltpu.VMEM((size_x, slots, slots), jnp.float32),
            pltpu.SMEM((size_x, size_z), jnp.int32),
            pltpu.SMEM((size_x, size_z), jnp.int32),
        ],
        compiler_params=pltpu.CompilerParams(vmem_limit_bytes=24 * 1024 * 1024),
    )(count2, own, low, high, far_low, far_high, velocity3, force3)
    return tuple(o.reshape(places.shape) for o in outs)


def solution(mesh):
    block = P(None, "gx", "gy", "gz", None)
    return jax.shard_map(
        per_device,
        mesh=mesh,
        in_specs=(
            block,
            block,
            block,
            P("gx", "gy", "gz"),
            P("gx", "gy", "gz", None),
            P("gx", "gy", "gz", None),
        ),
        out_specs=(block, block, block),
        check_vma=False,
    )
```

```python
import functools

import jax
import jax.numpy as jnp
from jax import lax
from jax.experimental import pallas as pl
from jax.experimental.pallas import tpu as pltpu
from jax.sharding import PartitionSpec as P

step_size = 0.005
cut_radius = 2.5
spacing = 1.1
edge_force = 24.0 * (2.0 * cut_radius ** (-13) - cut_radius ** (-7))

FAR = 1.0e6
NEAR = 1.0e5
MARGIN = 1.0e-3
ROWS = 32
GROUP = 8
ARRIVALS = 4
SHORT = 3
CHUNKS = 6
PART = 32
APART = 1.0e-2
COMBOS = [(dx, dy, dz) for dx in (-1, 0, 1) for dy in (-1, 0, 1) for dz in (-1, 0, 1)]
NEIGHBOURS = sorted(
    (c for c in COMBOS if c != (0, 0, 0)),
    key=lambda c: abs(c[0]) + abs(c[1]) + 2 * abs(c[2]),
)
BATCHES = 7


def cell_sides(slot_count):
    return (4.0 * spacing, 4.0 * spacing, spacing * (slot_count // 16))


def take(tile, index):
    return jnp.take_along_axis(tile, index, axis=1, mode="promise_in_bounds")


def rows_of(ref, c, x, size_z, slots):
    sub = lax.broadcasted_iota(jnp.int32, (size_z, slots), 0)
    tile = jnp.broadcast_to(ref[c, x, 0], (size_z, slots))
    for z in range(1, size_z):
        tile = jnp.where(sub == z, ref[c, x, z], tile)
    return tile


def pack_kernel(
    count_ref, atom_ref, face_ref, place_ref, velocity_ref, force_ref,
    slab_ref, first_ref, last_ref, half_ref,
):
    _, size_x, size_z, _, slots = place_ref.shape
    sides = cell_sides(slots)
    sub = lax.broadcasted_iota(jnp.int32, (size_z, slots), 0)
    lane = lax.broadcasted_iota(jnp.int32, (size_z, slots), 1)
    letter = slots - 6
    entries = atom_ref.shape[0]
    atoms = [atom_ref[e] for e in range(entries)]
    faces = [face_ref[e] for e in range(entries)]
    for x in range(size_x):
        count = jnp.zeros((size_z, slots), jnp.int32)
        for z in range(size_z):
            count = jnp.where(sub == z, count_ref[x, 0, z], count)
        first_atom = (x * size_z + sub) * slots
        leaving = jnp.full((size_z, slots), -1, jnp.int32)
        face = jnp.full((size_z, slots), -8, jnp.int32)
        for e in range(entries):
            offset = atoms[e] - first_atom
            here = (offset >= 0) & (offset < slots)
            leaving = jnp.where(here, offset, leaving)
            face = jnp.where(here, faces[e], face)
        any_leaves = leaving >= 0
        picked = jnp.maximum(leaving, 0)
        order = jnp.bitwise_xor(face, 1)
        axis_of = lax.shift_right_arithmetic(face, 1)
        sign = (2 * (face & 1) - 1).astype(jnp.float32)
        alive = (lane < count) & (lane != leaving)
        letter_lane = any_leaves & (lane == letter + order)
        speed_lane = lane == letter - 1
        letters = jnp.full((size_z, slots), FAR, jnp.float32)
        for c in range(3):
            half = rows_of(velocity_ref, c, x, size_z, slots) + (
                0.5 * step_size * rows_of(force_ref, c, x, size_z, slots)
            )
            drifted = rows_of(place_ref, c, x, size_z, slots) + step_size * half
            half_ref[c, x] = half
            moved = take(drifted, picked) - jnp.where(axis_of == c, sign * sides[c], 0.0)
            tile = jnp.where(alive, drifted, FAR)
            tile = jnp.where(letter_lane, moved, tile)
            tile = jnp.where(speed_lane, take(half, picked), tile)
            slab_ref[c, x] = tile
            first_ref[c, x] = tile[:1]
            last_ref[c, x] = tile[size_z - 1 :]
            letters = jnp.where(any_leaves & (lane == letter + order - 8 * c), moved, letters)
        slab_ref[3, x] = letters
        first_ref[3, x] = letters[:1]
        last_ref[3, x] = letters[size_z - 1 :]


def append_batch(batch, scanned, chunks, filled):
    rows, slots = filled.shape
    lane = lax.broadcasted_iota(jnp.int32, (rows, slots), 1)
    rank = (lane - filled) & (slots - 1)
    packed, start = scanned[0]
    place_shift = jnp.zeros((rows, slots), jnp.int32)
    local = rank
    picks = []
    for s in range(1, len(batch)):
        packed = packed | lax.shift_left(scanned[s][0], 8 * s)
        later = rank >= start
        picks.append(later)
        place_shift = jnp.where(later, 8 * s, place_shift)
        local = jnp.where(later, rank - start, local)
        start = start + scanned[s][1]
    position = jnp.zeros((rows, slots), jnp.int32)
    step = slots // 2
    while step >= 1:
        probe = take(packed, position + (step - 1))
        probe = lax.shift_right_logical(probe, place_shift) & 255
        position = jnp.where(probe <= local, position + step, position)
        step //= 2
    moved = []
    for c in range(3):
        value = take(batch[0][c], position)
        for s in range(1, len(batch)):
            value = jnp.where(picks[s - 1], take(batch[s][c], position), value)
        moved.append(value)
    chunk_id = lax.shift_right_logical(filled + rank, slots.bit_length() - 1)
    chunk_id = jnp.where(rank < start, chunk_id, -1)
    for k in range(len(chunks)):
        chosen = chunk_id == k
        chunks[k] = [jnp.where(chosen, moved[c], chunks[k][c]) for c in range(3)]
    return chunks, filled + start, start


def pair_force(own, other):
    total = [None, None, None]
    for row in other:
        delta = [own[c] - row[c] for c in range(3)]
        square = delta[0] * delta[0] + delta[1] * delta[1] + delta[2] * delta[2]
        root = lax.rsqrt(square)
        inverse = root * root
        fourth = inverse * inverse
        sixth = fourth * inverse
        strength = (48.0 * sixth - 24.0) * (fourth * fourth) - edge_force * root
        inside = (square < cut_radius * cut_radius) & (square > APART)
        strength = jnp.where(inside, strength, 0.0)
        for c in range(3):
            part = delta[c] * strength
            total[c] = part if total[c] is None else total[c] + part
    return total


def row_sums(found):
    return [jnp.sum(f, axis=1, keepdims=True) for f in found]


def force_kernel(
    count_ref,
    own_ref,
    low_ref,
    high_ref,
    far_low_ref,
    far_high_ref,
    half_ref,
    out_place_ref,
    out_velocity_ref,
    out_force_ref,
    comb,
    reach,
    cand,
    own_t,
    force_t,
    arrival_force,
    chunk_count,
    items,
    arrivals,
):
    _, ext_x, ext_z, slots = own_ref.shape
    size_x, size_z = ext_x - 2, ext_z - 2
    sides = cell_sides(slots)
    letter = slots - 6
    sub = lax.broadcasted_iota(jnp.int32, (ext_z, slots), 0)
    lane = lax.broadcasted_iota(jnp.int32, (ext_z, slots), 1)
    inner = (sub >= 1) & (sub <= size_z)
    far_tile = jnp.full((ext_z, slots), FAR, jnp.float32)
    planes = [low_ref, own_ref, high_ref]

    from_z_low = (lane == letter + 4) & (sub > 0)
    from_z_high = (lane == letter + 5) & (sub < ext_z - 1)
    for x in range(ext_x):
        for y in range(3):
            for c in range(3):
                tile = planes[y][c, x]
                out = jnp.where(lane < letter - 1, tile, FAR)
                if x > 0:
                    out = jnp.where(lane == letter, planes[y][c, x - 1], out)
                if x < ext_x - 1:
                    out = jnp.where(lane == letter + 1, planes[y][c, x + 1], out)
                below = planes[y - 1][c, x] if y > 0 else pltpu.roll(far_low_ref[x], 8 * c, 1)
                above = planes[y + 1][c, x] if y < 2 else pltpu.roll(far_high_ref[x], 8 * c, 1)
                out = jnp.where(lane == letter + 2, below, out)
                out = jnp.where(lane == letter + 3, above, out)
                out = jnp.where(from_z_low, pltpu.roll(tile, 1, 0), out)
                out = jnp.where(from_z_high, pltpu.roll(tile, ext_z - 1, 0), out)
                comb[c, x, y] = out

    lower, upper = [], []
    for c in range(3):
        low_tile = jnp.full((ext_z, slots), FAR, jnp.float32)
        high_tile = jnp.full((ext_z, slots), -FAR, jnp.float32)
        for x in range(1, size_x + 1):
            tile = own_ref[c, x]
            real = inner & (lane < letter - 1) & (tile < NEAR)
            low_tile = jnp.minimum(low_tile, jnp.where(real, tile, FAR))
            high_tile = jnp.maximum(high_tile, jnp.where(real, tile, -FAR))
        lower.append(jnp.min(low_tile, axis=(0, 1), keepdims=True) - (cut_radius + MARGIN))
        upper.append(jnp.max(high_tile, axis=(0, 1), keepdims=True) + (cut_radius + MARGIN))

    for x in range(ext_x):
        for y in range(3):
            for dz in (-1, 0, 1):
                tiles = [comb[c, x, y] for c in range(3)]
                if dz:
                    tiles = [pltpu.roll(t, (-dz) % ext_z, 0) for t in tiles]
                    tiles[2] = tiles[2] + dz * sides[2]
                usable = inner
                if dz:
                    usable = usable & ((tiles[2] > lower[2]) if dz < 0 else (tiles[2] < upper[2]))
                if y != 1:
                    tiles[1] = tiles[1] + (y - 1) * sides[1]
                    usable = usable & ((tiles[1] > lower[1]) if y == 0 else (tiles[1] < upper[1]))
                reach[dz + 1, 0, x, y] = jnp.where(usable, tiles[0], FAR)
                reach[dz + 1, 1, x, y] = tiles[1]
                reach[dz + 1, 2, x, y] = tiles[2]

    row_id = lax.broadcasted_iota(jnp.int32, (slots, 2 * slots), 0)
    col_id = lax.broadcasted_iota(jnp.int32, (slots, 2 * slots), 1)
    weights = jnp.where(row_id <= col_id, 1.0, 0.0).astype(jnp.bfloat16)
    excess = jnp.full((ext_z, slots), -1, jnp.int32)
    counts = []
    for x in range(size_x):
        count = jnp.zeros((ext_z, slots), jnp.int32)
        for z in range(size_z):
            count = jnp.where(sub == z + 1, count_ref[x, 0, z], count)
        counts.append(count)

    chunk_tiles = []
    for x in range(size_x):
        center = [comb[c, x + 1, 1] for c in range(3)]
        sources = [(inner & (lane >= letter) & (center[0] < NEAR), center)]
        for dx, dy, dz in NEIGHBOURS:
            tiles = [reach[dz + 1, c, x + 1 + dx, 1 + dy] for c in range(3)]
            real = tiles[0] < NEAR
            if dx:
                tiles[0] = tiles[0] + dx * sides[0]
                real = real & ((tiles[0] > lower[0]) if dx < 0 else (tiles[0] < upper[0]))
            sources.append((real, tiles))
        masks = jnp.concatenate([jnp.where(m, 1.0, 0.0) for m, _ in sources], axis=0)
        scanned = jnp.dot(
            masks.astype(jnp.bfloat16), weights, preferred_element_type=jnp.float32
        ).astype(jnp.int32)
        split = []
        for s in range(len(sources)):
            part = scanned[ext_z * s : ext_z * (s + 1)]
            split.append((part[:, :slots], part[:, slots:]))
        chunks = [[jnp.where(lane < counts[x], t, FAR) for t in center]]
        chunks += [[far_tile] * 3 for _ in range(CHUNKS - 1)]
        filled = counts[x]
        for batch in range(BATCHES):
            ids = range(batch, len(sources), BATCHES)
            chunks, filled, added = append_batch(
                [sources[s][1] for s in ids], [split[s] for s in ids], chunks, filled
            )
            excess = jnp.maximum(excess, added - slots)
        excess = jnp.maximum(excess, filled - CHUNKS * slots)
        for k in range(CHUNKS):
            for c in range(3):
                cand[x, k, c] = chunks[k][c]
        chunk_tiles.append(lax.shift_right_logical(filled + (slots - 1), slots.bit_length() - 1))

    overflow = jnp.max(excess.astype(jnp.float32)) > 0.0
    longest = functools.reduce(jnp.maximum, chunk_tiles)
    longest = jnp.max(jnp.where(inner, longest, 0).astype(jnp.float32)) > SHORT
    position = 0
    for x in range(size_x):
        for z in range(size_z):
            chunk_count[x, z] = jnp.where(overflow, len(COMBOS), chunk_tiles[x][z + 1, 0])
            code = x * 256 + z * 16
            for block in range(slots // 8):
                items[position + block] = code + block
            position = position + lax.shift_right_logical(count_ref[x, 0, z] + 7, 3)
    item_steps = lax.div(position + (GROUP - 1), GROUP)
    for extra in range(GROUP):
        items[position + extra] = slots // 8 - 1
    position = 0
    for x in range(size_x):
        arrived = jnp.zeros((ext_z, slots), jnp.float32)
        for o in range(6):
            arrived = jnp.where(lane == letter + o, float(2**o), arrived)
        arrived = jnp.where(comb[0, x + 1, 1] < NEAR, arrived, 0.0)
        arrived = jnp.sum(arrived, axis=1, keepdims=True).astype(jnp.int32)
        for z in range(size_z):
            bits = arrived[z + 1, 0]
            for o in range(6):
                arrivals[position] = x * 256 + z * 16 + o
                position = position + (lax.shift_right_logical(bits, o) & 1)
    arrival_steps = lax.div(position + (ARRIVALS - 1), ARRIVALS)
    for extra in range(ARRIVALS):
        arrivals[position + extra] = 7

    @pl.when(overflow)
    def _():
        for k, (dx, dy, dz) in enumerate(COMBOS):
            for x in range(size_x):
                for c, step in enumerate((dx, dy, dz)):
                    tile = comb[c, x + 1 + dx, 1 + dy]
                    if dz:
                        tile = pltpu.roll(tile, (-dz) % ext_z, 0)
                    cand[x, k, c] = tile + step * sides[c]

    for x in range(size_x):
        parts = []
        rest = [comb[c, x + 1, 1] for c in range(3)]
        for _ in range(3):
            rounded = [r.astype(jnp.bfloat16).astype(jnp.float32) for r in rest]
            rest = [r - h for r, h in zip(rest, rounded)]
            parts += rounded + [jnp.zeros((PART - 3 * ext_z, slots), jnp.float32)]
        parts.append(jnp.zeros((slots - 3 * PART, slots), jnp.float32))
        own_t[x] = jnp.concatenate(parts, axis=0).T
        force_t[x] = jnp.zeros((slots, slots), jnp.float32)

    for x in range(size_x):
        for c in range(3):
            arrival_force[x, c] = jnp.zeros((ext_z, slots), jnp.float32)

    row_id = lax.broadcasted_iota(jnp.int32, (slots, 3 * slots), 0)
    col_id = lax.broadcasted_iota(jnp.int32, (slots, 3 * slots), 1)
    of_axis = lax.shift_right_logical(row_id & (PART - 1), 3)
    spread = (of_axis == lax.shift_right_logical(col_id, 7)) & (row_id < 3 * PART)
    spread = jnp.where(spread, 1.0, 0.0).astype(jnp.bfloat16)
    summing = jnp.ones((2 * slots, slots), jnp.bfloat16)

    def each_group(group, carry):
        work, held = [], []
        for g in range(GROUP):
            code = items[group * GROUP + g]
            x = lax.shift_right_logical(code, 8)
            z = lax.shift_right_logical(code, 4) & 15
            rows = pl.ds(pl.multiple_of((code & 15) * 8, 8), 8)
            held.append(jnp.where((lane & 7) == z + 1, own_t[x, rows, :], 0.0))
            work.append((x, z, rows))
        columns = jnp.dot(
            jnp.concatenate(held, axis=0).astype(jnp.bfloat16),
            spread,
            preferred_element_type=jnp.float32,
        )
        found = []
        for g, (x, z, _) in enumerate(work):
            own = [columns[8 * g : 8 * g + 8, c * slots : (c + 1) * slots] for c in range(3)]
            other = [
                [cand[x, k, c, pl.ds(z + 1, 1), :] for c in range(3)] for k in range(SHORT)
            ]
            found += pair_force(own, other)
        found = jnp.concatenate(found, axis=0)
        rounded = found.astype(jnp.bfloat16)
        rest = (found - rounded.astype(jnp.float32)).astype(jnp.bfloat16)
        found = jnp.dot(
            jnp.concatenate([rounded, rest], axis=1), summing, preferred_element_type=jnp.float32
        )
        for g, (x, z, rows) in enumerate(work):
            result = force_t[x, rows, :]
            for c in range(3):
                start = (3 * g + c) * 8
                result = jnp.where(lane == c * ext_z + z + 1, found[start : start + 8], result)
            force_t[x, rows, :] = result
        return carry

    lax.fori_loop(0, item_steps, each_group, 0)

    def each_arrival(group, carry):
        work = []
        for g in range(ARRIVALS):
            code = arrivals[group * ARRIVALS + g]
            x = lax.shift_right_logical(code, 8)
            z = lax.shift_right_logical(code, 4) & 15
            slot = letter + (code & 15)
            pick = jnp.full((ext_z, slots), slot & (slots - 1), jnp.int32)
            own = []
            for c in range(3):
                row = comb[c, x + 1, 1, pl.ds(z + 1, 1), :]
                own.append(take(jnp.broadcast_to(row, (ext_z, slots)), pick))
            away = sub - (z + 1)
            rise = away.astype(jnp.float32) * sides[2]
            beside = jnp.abs(away) <= 1
            other = []
            for dx in (-1, 0, 1):
                for dy in (-1, 0, 1):
                    tiles = [comb[c, x + 1 + dx, 1 + dy] for c in range(3)]
                    tiles[0] = jnp.where(beside, tiles[0], FAR)
                    tiles[0] = tiles[0] + dx * sides[0] if dx else tiles[0]
                    tiles[1] = tiles[1] + dy * sides[1] if dy else tiles[1]
                    tiles[2] = tiles[2] + rise
                    other.append(tiles)
            found = row_sums(pair_force(own, other))
            found = [jnp.sum(f, axis=0, keepdims=True) for f in found]
            work.append((x, (sub == z + 1) & (lane == slot), found))
        for x, spot, found in work:
            for c in range(3):
                arrival_force[x, c] = jnp.where(spot, found[c], arrival_force[x, c])
        return carry

    lax.fori_loop(0, arrival_steps, each_arrival, 0)

    lane_rows = lax.broadcasted_iota(jnp.int32, (ROWS, slots), 1)
    row_shift = ROWS.bit_length() - 1

    @pl.when(overflow | longest)
    def _():
        def each_x(x, carry):
            for z in range(size_z):
                picks = [c * ext_z + z + 1 for c in range(3)]
                blocks = lax.shift_right_logical(count_ref[x, 0, z] + (ROWS - 1), row_shift)

                def each_chunk(k, chunk_carry):
                    def each_block(block, block_carry):
                        rows = pl.ds(pl.multiple_of(block * ROWS, ROWS), ROWS)
                        held = own_t[x, rows, :]
                        own = []
                        for p in picks:
                            parts = [held[:, p + PART * i : p + PART * i + 1] for i in range(3)]
                            own.append(parts[0] + parts[1] + parts[2])
                        chunk = [cand[x, k, c, z + 1 : z + 2, :] for c in range(3)]
                        found = row_sums(pair_force(own, [chunk]))
                        result = force_t[x, rows, :]
                        for c in range(3):
                            result = jnp.where(lane_rows == picks[c], result + found[c], result)
                        force_t[x, rows, :] = result
                        return block_carry

                    return lax.fori_loop(0, blocks, each_block, chunk_carry)

                lax.fori_loop(SHORT, chunk_count[x, z], each_chunk, 0)
            return carry

        lax.fori_loop(0, size_x, each_x, 0)

    speed = jnp.full((ext_z, slots), letter - 1, jnp.int32)
    for x in range(size_x):
        turned = force_t[x].T
        count = counts[x]
        base = comb[0, x + 1, 1]
        filled = count
        index = lane
        for o in range(6):
            valid = take(base, jnp.full((ext_z, slots), letter + o, jnp.int32)) < NEAR
            index = jnp.where(valid & (lane == filled), letter + o, index)
            filled = filled + jnp.where(valid, 1, 0)
        placed = take(base, index)
        alive = (lane < filled) & (placed < NEAR)
        for c in range(3):
            half = half_ref[c, x]
            blank = jnp.zeros((1, slots), jnp.float32)
            half = jnp.concatenate([blank, half, blank], axis=0)
            tile = own_ref[c, x + 1]
            sent = [
                own_ref[c, x],
                own_ref[c, x + 2],
                low_ref[c, x + 1],
                high_ref[c, x + 1],
                pltpu.roll(tile, 1, 0),
                pltpu.roll(tile, ext_z - 1, 0),
            ]
            for o in range(6):
                half = jnp.where(lane == letter + o, take(sent[o], speed), half)
            where_to = placed if c == 0 else take(comb[c, x + 1, 1], index)
            force = turned[c * ext_z : (c + 1) * ext_z]
            force = jnp.where(lane >= letter, arrival_force[x, c], force)
            force = jnp.where(alive, take(force, index), 0.0)
            half = take(half, index) + 0.5 * step_size * force
            where_to = jnp.where(alive, where_to, 0.0)
            half = jnp.where(alive, half, 0.0)
            for z in range(size_z):
                out_place_ref[c, x, z] = where_to[z + 1 : z + 2]
                out_velocity_ref[c, x, z] = half[z + 1 : z + 2]
                out_force_ref[c, x, z] = force[z + 1 : z + 2]


def shifted(value, axis, steps):
    count = lax.axis_size(axis)
    return lax.ppermute(value, axis, [(i, (i + steps) % count) for i in range(count)])


def per_device(places, velocity, forces_old, counts, mig_atom, mig_face):
    size_x, size_y, size_z, slots = places.shape[1:]
    assert size_y == 1 and size_z == 6 and slots == 128 and size_x >= 2
    flat = (size_x, size_z, slots)
    swapped = [jnp.transpose(a, (0, 1, 3, 2, 4)) for a in (places, velocity, forces_old)]
    vmem = pl.BlockSpec(memory_space=pltpu.VMEM)
    smem = pl.BlockSpec(memory_space=pltpu.SMEM)
    slab, first, last, half = pl.pallas_call(
        pack_kernel,
        out_shape=[
            jax.ShapeDtypeStruct((4,) + flat, jnp.float32),
            jax.ShapeDtypeStruct((4, size_x, 1, slots), jnp.float32),
            jax.ShapeDtypeStruct((4, size_x, 1, slots), jnp.float32),
            jax.ShapeDtypeStruct((3,) + flat, jnp.float32),
        ],
        in_specs=[smem] * 3 + [vmem] * 3,
        out_specs=[vmem] * 4,
    )(counts, mig_atom.reshape(-1), mig_face.reshape(-1), *swapped)

    from_low = shifted(last, "gz", 1)
    from_high = shifted(first, "gz", -1)
    slab = jnp.concatenate([from_low, slab, from_high], axis=2)
    if lax.axis_size("gx") == 2:
        both = shifted(jnp.concatenate([slab[:, :1], slab[:, size_x - 1 :]], axis=1), "gx", 1)
        from_low, from_high = both[:, 1:], both[:, :1]
    else:
        from_low = shifted(slab[:, size_x - 1 :], "gx", 1)
        from_high = shifted(slab[:, :1], "gx", -1)
    slab = jnp.concatenate([from_low, slab, from_high], axis=1)
    own, letters = slab[:3], slab[3]
    low = shifted(own, "gy", 1)
    high = shifted(own, "gy", -1)
    far_low = shifted(letters, "gy", 2)
    far_high = far_low if lax.axis_size("gy") == 4 else shifted(letters, "gy", -2)

    ext_x, ext_z = size_x + 2, size_z + 2
    outs = pl.pallas_call(
        force_kernel,
        out_shape=[jax.ShapeDtypeStruct(swapped[0].shape, jnp.float32)] * 3,
        in_specs=[smem] + [vmem] * 6,
        out_specs=[vmem] * 3,
        scratch_shapes=[
            pltpu.VMEM((3, ext_x, 3, ext_z, slots), jnp.float32),
            pltpu.VMEM((3, 3, ext_x, 3, ext_z, slots), jnp.float32),
            pltpu.VMEM((size_x, len(COMBOS), 3, ext_z, slots), jnp.float32),
            pltpu.VMEM((size_x, slots, slots), jnp.float32),
            pltpu.VMEM((size_x, slots, slots), jnp.float32),
            pltpu.VMEM((size_x, 3, ext_z, slots), jnp.float32),
            pltpu.SMEM((size_x, size_z), jnp.int32),
            pltpu.SMEM((size_x * size_z * (slots // 8) + GROUP,), jnp.int32),
            pltpu.SMEM((size_x * size_z * 6 + ARRIVALS,), jnp.int32),
        ],
        compiler_params=pltpu.CompilerParams(vmem_limit_bytes=24 * 1024 * 1024),
    )(counts, own, low, high, far_low, far_high, half)
    return tuple(jnp.transpose(o, (0, 1, 3, 2, 4)) for o in outs)


def solution(mesh):
    block = P(None, "gx", "gy", "gz", None)
    return jax.shard_map(
        per_device,
        mesh=mesh,
        in_specs=(
            block,
            block,
            block,
            P("gx", "gy", "gz"),
            P("gx", "gy", "gz", None),
            P("gx", "gy", "gz", None),
        ),
        out_specs=(block, block, block),
        check_vma=False,
    )
```

```python
import functools

import jax
import jax.numpy as jnp
from jax import lax
from jax.experimental import pallas as pl
from jax.experimental.pallas import tpu as pltpu
from jax.sharding import PartitionSpec as P

step_size = 0.005
cut_radius = 2.5
spacing = 1.1
edge_force = 24.0 * (2.0 * cut_radius ** (-13) - cut_radius ** (-7))

FAR = 24.0
NEAR = 16.0
MARGIN = 1.0e-3
GROUP = 48
ARRIVALS = 4
SHORT = 2
CHUNKS = 6
PLANE_CHUNKS = 3
PART = 32
APART = 0.25
COMBOS = [(dx, dy, dz) for dx in (-1, 0, 1) for dy in (-1, 0, 1) for dz in (-1, 0, 1)]


def by_weight(combos):
    return sorted(combos, key=lambda c: abs(c[0]) + abs(c[1]) + 2 * abs(c[2]))


PLANE = by_weight(c for c in COMBOS if c[1] == 0 and c != (0, 0, 0))
SIDES = by_weight(c for c in COMBOS if c[1] != 0)


def cell_sides(slot_count):
    return (4.0 * spacing, 4.0 * spacing, spacing * (slot_count // 16))


def take(tile, index):
    return jnp.take_along_axis(tile, index, axis=1, mode="promise_in_bounds")


def rows_of(ref, c, x, size_z, slots):
    sub = lax.broadcasted_iota(jnp.int32, (size_z, slots), 0)
    tile = jnp.broadcast_to(ref[c, x, 0], (size_z, slots))
    for z in range(1, size_z):
        tile = jnp.where(sub == z, ref[c, x, z], tile)
    return tile


def pack_kernel(
    count_ref, atom_ref, face_ref, place_ref, velocity_ref, force_ref,
    slab_ref, first_ref, last_ref, half_ref,
):
    _, size_x, size_z, _, slots = place_ref.shape
    sides = cell_sides(slots)
    sub = lax.broadcasted_iota(jnp.int32, (size_z, slots), 0)
    lane = lax.broadcasted_iota(jnp.int32, (size_z, slots), 1)
    letter = slots - 6
    entries = atom_ref.shape[0]
    atoms = [atom_ref[e] for e in range(entries)]
    faces = [face_ref[e] for e in range(entries)]
    for x in range(size_x):
        count = jnp.zeros((size_z, slots), jnp.int32)
        for z in range(size_z):
            count = jnp.where(sub == z, count_ref[x, 0, z], count)
        first_atom = (x * size_z + sub) * slots
        leaving = jnp.full((size_z, slots), -1, jnp.int32)
        face = jnp.full((size_z, slots), -8, jnp.int32)
        for e in range(entries):
            offset = atoms[e] - first_atom
            here = (offset >= 0) & (offset < slots)
            leaving = jnp.where(here, offset, leaving)
            face = jnp.where(here, faces[e], face)
        any_leaves = leaving >= 0
        picked = jnp.maximum(leaving, 0)
        order = jnp.bitwise_xor(face, 1)
        axis_of = lax.shift_right_arithmetic(face, 1)
        sign = (2 * (face & 1) - 1).astype(jnp.float32)
        alive = (lane < count) & (lane != leaving)
        letter_lane = any_leaves & (lane == letter + order)
        speed_lane = lane == letter - 1
        letters = jnp.full((size_z, slots), FAR, jnp.float32)
        for c in range(3):
            half = rows_of(velocity_ref, c, x, size_z, slots) + (
                0.5 * step_size * rows_of(force_ref, c, x, size_z, slots)
            )
            drifted = rows_of(place_ref, c, x, size_z, slots) + step_size * half
            half_ref[c, x] = half
            moved = take(drifted, picked) - jnp.where(axis_of == c, sign * sides[c], 0.0)
            tile = jnp.where(alive, drifted, FAR)
            tile = jnp.where(letter_lane, moved, tile)
            tile = jnp.where(speed_lane, take(half, picked), tile)
            slab_ref[c, x] = tile
            first_ref[c, x] = tile[:1]
            last_ref[c, x] = tile[size_z - 1 :]
            letters = jnp.where(any_leaves & (lane == letter + order - 8 * c), moved, letters)
        slab_ref[3, x] = letters
        first_ref[3, x] = letters[:1]
        last_ref[3, x] = letters[size_z - 1 :]


def append_batch(batch, scanned, chunks, filled):
    rows, slots = filled.shape
    lane = lax.broadcasted_iota(jnp.int32, (rows, slots), 1)
    rank = (lane - filled) & (slots - 1)
    packed, start = scanned[0]
    place_shift = jnp.zeros((rows, slots), jnp.int32)
    local = rank
    picks = []
    for s in range(1, len(batch)):
        packed = packed | lax.shift_left(scanned[s][0], 8 * s)
        later = rank >= start
        picks.append(later)
        place_shift = jnp.where(later, 8 * s, place_shift)
        local = jnp.where(later, rank - start, local)
        start = start + scanned[s][1]
    position = jnp.zeros((rows, slots), jnp.int32)
    step = slots // 2
    while step >= 1:
        probe = take(packed, position + (step - 1))
        probe = lax.shift_right_logical(probe, place_shift) & 255
        position = jnp.where(probe <= local, position + step, position)
        step //= 2
    moved = []
    for c in range(3):
        value = take(batch[0][c], position)
        for s in range(1, len(batch)):
            value = jnp.where(picks[s - 1], take(batch[s][c], position), value)
        moved.append(value)
    chunk_id = lax.shift_right_logical(filled + rank, slots.bit_length() - 1)
    chunk_id = jnp.where(rank < start, chunk_id, -1)
    for k in range(len(chunks)):
        chosen = chunk_id == k
        chunks[k] = [jnp.where(chosen, moved[c], chunks[k][c]) for c in range(3)]
    return chunks, filled + start, start


def pair_force(own, other):
    total = [None, None, None]
    for row in other:
        delta = [own[c] - row[c] for c in range(3)]
        square = delta[0] * delta[0] + delta[1] * delta[1] + delta[2] * delta[2]
        square = jnp.minimum(jnp.maximum(square, APART), cut_radius * cut_radius)
        root = lax.rsqrt(square)
        inverse = root * root
        fourth = inverse * inverse
        sixth = fourth * inverse
        strength = (sixth - 0.5) * (fourth * fourth) - (edge_force / 48.0) * root
        for c in range(3):
            part = delta[c] * strength
            total[c] = part if total[c] is None else total[c] + part
    return total


def row_sums(found):
    return [jnp.sum(f, axis=1, keepdims=True) for f in found]


def scan_weights(slots):
    row_id = lax.broadcasted_iota(jnp.int32, (slots, 2 * slots), 0)
    col_id = lax.broadcasted_iota(jnp.int32, (slots, 2 * slots), 1)
    return jnp.where(row_id <= col_id, 1.0, 0.0).astype(jnp.bfloat16)


def append_sources(sources, chunks, filled, excess, weights):
    slots = weights.shape[0]
    rows = filled.shape[0]
    masks = jnp.concatenate([jnp.where(m, 1.0, 0.0) for m, _ in sources], axis=0)
    scanned = jnp.dot(
        masks.astype(jnp.bfloat16), weights, preferred_element_type=jnp.float32
    ).astype(jnp.int32)
    split = []
    for s in range(len(sources)):
        part = scanned[rows * s : rows * (s + 1)]
        split.append((part[:, :slots], part[:, slots:]))
    batches = -(-len(sources) // 4)
    for batch in range(batches):
        ids = range(batch, len(sources), batches)
        chunks, filled, added = append_batch(
            [sources[s][1] for s in ids], [split[s] for s in ids], chunks, filled
        )
        excess = jnp.maximum(excess, added - slots)
    return chunks, filled, jnp.maximum(excess, filled - len(chunks) * slots)


def sideways(tiles, dx, side, lower, upper):
    real = tiles[0] < NEAR
    if dx:
        tiles = [tiles[0] + dx * side] + tiles[1:]
        real = real & ((tiles[0] > lower) if dx < 0 else (tiles[0] < upper))
    return real, tiles


def pair_loop(items, steps, own_ref, cand, chunk_ids, force_ref, slots, ext_z):
    lane = lax.broadcasted_iota(jnp.int32, (8, slots), 1)
    shift = slots.bit_length() - 1
    row_id = lax.broadcasted_iota(jnp.int32, (slots, 3 * slots), 0)
    col_id = lax.broadcasted_iota(jnp.int32, (slots, 3 * slots), 1)
    of_axis = lax.shift_right_logical(row_id & (PART - 1), 3)
    spread = (of_axis == lax.shift_right_logical(col_id, shift)) & (row_id < 3 * PART)
    spread = jnp.where(spread, 1.0, 0.0).astype(jnp.bfloat16)
    row_id = lax.broadcasted_iota(jnp.int32, (3 * slots, slots), 0)
    col_id = lax.broadcasted_iota(jnp.int32, (3 * slots, slots), 1) - 3 * PART
    summing = (lax.shift_right_arithmetic(col_id, 3) == lax.shift_right_logical(row_id, shift))
    summing = jnp.where(summing, 1.0, 0.0).astype(jnp.bfloat16)
    summing = jnp.concatenate([summing, summing], axis=0)

    def each_group(group, carry):
        work, held = [], []
        for g in range(GROUP):
            code = items[group * GROUP + g]
            x = lax.shift_right_logical(code, 8) & 15
            z = lax.shift_right_logical(code, 4) & 15
            first = lax.shift_right_logical(code, 12)
            rows = pl.ds(pl.multiple_of((code & 15) * 8, 8), 8)
            mask = (lane & 7) == z + 1
            held.append(jnp.where(mask, own_ref[x, rows, :], 0.0))
            work.append((x, z, first, rows, mask))
        columns = jnp.dot(
            jnp.concatenate(held, axis=0).astype(jnp.bfloat16),
            spread,
            preferred_element_type=jnp.float32,
        )
        found = []
        for g, (x, z, first, _, _) in enumerate(work):
            own = [columns[8 * g : 8 * g + 8, c * slots : (c + 1) * slots] for c in range(3)]
            other = [
                [cand[x, first + k, c, pl.ds(z + 1, 1), :] for c in range(3)] for k in chunk_ids
            ]
            found.append(pair_force(own, other))
        found = [jnp.concatenate([f[c] for f in found], axis=0) for c in range(3)]
        rounded = [f.astype(jnp.bfloat16) for f in found]
        rest = [(f - r.astype(jnp.float32)).astype(jnp.bfloat16) for f, r in zip(found, rounded)]
        sums = jnp.dot(
            jnp.concatenate(rounded + rest, axis=1), summing, preferred_element_type=jnp.float32
        )
        for g, (x, _, _, rows, mask) in enumerate(work):
            force_ref[x, rows, :] = force_ref[x, rows, :] + jnp.where(
                mask, sums[8 * g : 8 * g + 8], 0.0
            )
        return carry

    lax.fori_loop(0, steps, each_group, 0)


def plane_kernel(
    count_ref, own_ref, own_t, begun, filled_ref, box_ref, excess_ref, items, steps_ref,
    reach, cand,
):
    _, ext_x, ext_z, slots = own_ref.shape
    size_x, size_z = ext_x - 2, ext_z - 2
    sides = cell_sides(slots)
    letter = slots - 6
    sub = lax.broadcasted_iota(jnp.int32, (ext_z, slots), 0)
    lane = lax.broadcasted_iota(jnp.int32, (ext_z, slots), 1)
    inner = (sub >= 1) & (sub <= size_z)
    stayed = lane < letter - 1
    far_tile = jnp.full((ext_z, slots), FAR, jnp.float32)

    position = 0
    for x in range(size_x):
        for z in range(size_z):
            code = x * 256 + z * 16
            for block in range(slots // 8):
                items[position + block] = code + block
            position = position + lax.shift_right_logical(count_ref[x, 0, z] + 7, 3)
    steps_ref[0] = lax.div(position + (GROUP - 1), GROUP)
    for extra in range(GROUP):
        items[position + extra] = slots // 8 - 1

    lower, upper = [], []
    for c in range(3):
        low_tile = jnp.full((ext_z, slots), FAR, jnp.float32)
        high_tile = jnp.full((ext_z, slots), -FAR, jnp.float32)
        for x in range(1, size_x + 1):
            tile = own_ref[c, x]
            real = inner & stayed & (tile < NEAR)
            low_tile = jnp.minimum(low_tile, jnp.where(real, tile, FAR))
            high_tile = jnp.maximum(high_tile, jnp.where(real, tile, -FAR))
        lower.append(jnp.min(low_tile, axis=(0, 1), keepdims=True) - (cut_radius + MARGIN))
        upper.append(jnp.max(high_tile, axis=(0, 1), keepdims=True) + (cut_radius + MARGIN))
        box_ref[c] = jnp.broadcast_to(lower[c], (ext_z, slots))
        box_ref[3 + c] = jnp.broadcast_to(upper[c], (ext_z, slots))

    centers = {}
    from_z_low = (lane == letter + 4) & (sub > 0)
    from_z_high = (lane == letter + 5) & (sub < ext_z - 1)
    for x in range(ext_x):
        settled = []
        for c in range(3):
            tile = own_ref[c, x]
            out = jnp.where(stayed, tile, FAR)
            if x > 0:
                out = jnp.where(lane == letter, own_ref[c, x - 1], out)
            if x < ext_x - 1:
                out = jnp.where(lane == letter + 1, own_ref[c, x + 1], out)
            out = jnp.where(from_z_low, pltpu.roll(tile, 1, 0), out)
            settled.append(jnp.where(from_z_high, pltpu.roll(tile, ext_z - 1, 0), out))
        centers[x] = settled
        for dz in (-1, 0, 1):
            tiles = settled
            usable = inner
            if dz:
                tiles = [pltpu.roll(t, (-dz) % ext_z, 0) for t in tiles]
                tiles[2] = tiles[2] + dz * sides[2]
                usable = usable & ((tiles[2] > lower[2]) if dz < 0 else (tiles[2] < upper[2]))
            reach[dz + 1, 0, x] = jnp.where(usable, tiles[0], FAR)
            reach[dz + 1, 1, x] = tiles[1]
            reach[dz + 1, 2, x] = tiles[2]

    for x in range(size_x):
        parts = []
        rest = [jnp.where(stayed, own_ref[c, x + 1], FAR) for c in range(3)]
        for _ in range(3):
            rounded = [r.astype(jnp.bfloat16).astype(jnp.float32) for r in rest]
            rest = [r - h for r, h in zip(rest, rounded)]
            parts += rounded + [jnp.zeros((PART - 3 * ext_z, slots), jnp.float32)]
        parts.append(jnp.zeros((slots - 3 * PART, slots), jnp.float32))
        own_t[x] = jnp.concatenate(parts, axis=0).T

    weights = scan_weights(slots)
    excess = jnp.full((ext_z, slots), -1, jnp.int32)
    for x in range(size_x):
        count = jnp.zeros((ext_z, slots), jnp.int32)
        for z in range(size_z):
            count = jnp.where(sub == z + 1, count_ref[x, 0, z], count)
        center = centers[x + 1]
        sources = [(inner & (lane >= letter) & (center[0] < NEAR), center)]
        for dx, _, dz in PLANE:
            tiles = [reach[dz + 1, c, x + 1 + dx] for c in range(3)]
            sources.append(sideways(tiles, dx, sides[0], lower[0], upper[0]))
        chunks = [[jnp.where(lane < count, t, FAR) for t in center]]
        chunks += [[far_tile] * 3 for _ in range(PLANE_CHUNKS - 1)]
        chunks, filled, excess = append_sources(sources, chunks, count, excess, weights)
        filled_ref[x] = jnp.maximum(filled - slots, 0)
        for c in range(3):
            cand[x, 0, c] = chunks[0][c]
            for k in range(PLANE_CHUNKS - 1):
                begun[x, k, c] = chunks[k + 1][c]
    excess_ref[...] = excess
    pair_loop(items, steps_ref[0], own_t, cand, (0,), own_t, slots, ext_z)


def force_kernel(
    count_ref,
    items,
    steps_ref,
    own_ref,
    low_ref,
    high_ref,
    far_low_ref,
    far_high_ref,
    half_ref,
    own_t,
    begun,
    filled_ref,
    box_ref,
    excess_ref,
    out_place_ref,
    out_velocity_ref,
    out_force_ref,
    comb,
    reach,
    cand,
    force_t,
    arrival_force,
    chunk_count,
    arrivals,
    more_items,
):
    _, ext_x, ext_z, slots = own_ref.shape
    size_x, size_z = ext_x - 2, ext_z - 2
    sides = cell_sides(slots)
    letter = slots - 6
    sub = lax.broadcasted_iota(jnp.int32, (ext_z, slots), 0)
    lane = lax.broadcasted_iota(jnp.int32, (ext_z, slots), 1)
    inner = (sub >= 1) & (sub <= size_z)
    far_tile = jnp.full((ext_z, slots), FAR, jnp.float32)
    planes = [low_ref, own_ref, high_ref]
    lower = [box_ref[c] for c in range(3)]
    upper = [box_ref[3 + c] for c in range(3)]

    from_z_low = (lane == letter + 4) & (sub > 0)
    from_z_high = (lane == letter + 5) & (sub < ext_z - 1)
    for x in range(ext_x):
        for y in range(3):
            for c in range(3):
                tile = planes[y][c, x]
                out = jnp.where(lane < letter - 1, tile, FAR)
                if x > 0:
                    out = jnp.where(lane == letter, planes[y][c, x - 1], out)
                if x < ext_x - 1:
                    out = jnp.where(lane == letter + 1, planes[y][c, x + 1], out)
                below = planes[y - 1][c, x] if y > 0 else pltpu.roll(far_low_ref[x], 8 * c, 1)
                above = planes[y + 1][c, x] if y < 2 else pltpu.roll(far_high_ref[x], 8 * c, 1)
                out = jnp.where(lane == letter + 2, below, out)
                out = jnp.where(lane == letter + 3, above, out)
                out = jnp.where(from_z_low, pltpu.roll(tile, 1, 0), out)
                out = jnp.where(from_z_high, pltpu.roll(tile, ext_z - 1, 0), out)
                comb[c, x, y] = out

    spare = lane == letter - 2
    for x in range(ext_x):
        for side, y in enumerate((0, 2)):
            crossed = [
                pltpu.roll(planes[y][c, x], slots - 4 - side, 1) for c in range(3)
            ]
            settled = [comb[c, x, y] for c in range(3)]
            settled[1] = settled[1] + (y - 1) * sides[1]
            settled = [jnp.where(spare, a, b) for a, b in zip(crossed, settled)]
            reached = (settled[1] > lower[1]) if y == 0 else (settled[1] < upper[1])
            settled[0] = jnp.where(reached, settled[0], FAR)
            for dz in (-1, 0, 1):
                tiles = settled
                usable = inner
                if dz:
                    tiles = [pltpu.roll(t, (-dz) % ext_z, 0) for t in tiles]
                    tiles[2] = tiles[2] + dz * sides[2]
                    usable = usable & ((tiles[2] > lower[2]) if dz < 0 else (tiles[2] < upper[2]))
                reach[dz + 1, 0, x, side] = jnp.where(usable, tiles[0], FAR)
                reach[dz + 1, 1, x, side] = tiles[1]
                reach[dz + 1, 2, x, side] = tiles[2]

    weights = scan_weights(slots)
    excess = excess_ref[...]
    counts = []
    for x in range(size_x):
        count = jnp.zeros((ext_z, slots), jnp.int32)
        for z in range(size_z):
            count = jnp.where(sub == z + 1, count_ref[x, 0, z], count)
        counts.append(count)

    chunk_tiles = []
    for x in range(size_x):
        sources = []
        for dx, dy, dz in SIDES:
            tiles = [reach[dz + 1, c, x + 1 + dx, (dy + 1) // 2] for c in range(3)]
            sources.append(sideways(tiles, dx, sides[0], lower[0], upper[0]))
        chunks = [[begun[x, k, c] for c in range(3)] for k in range(PLANE_CHUNKS - 1)]
        chunks += [[far_tile] * 3 for _ in range(CHUNKS - PLANE_CHUNKS + 1)]
        chunks, filled, excess = append_sources(sources, chunks, filled_ref[x], excess, weights)
        for k in range(CHUNKS):
            for c in range(3):
                cand[x, k, c] = chunks[k][c]
        chunk_tiles.append(lax.shift_right_logical(filled + (slots - 1), slots.bit_length() - 1))

    overflow = jnp.max(excess.astype(jnp.float32)) > 0.0
    longest = functools.reduce(jnp.maximum, chunk_tiles)
    longest = jnp.max(jnp.where(inner, longest, 0).astype(jnp.float32)) > SHORT
    for x in range(size_x):
        for z in range(size_z):
            chunk_count[x, z] = jnp.where(overflow, len(COMBOS), chunk_tiles[x][z + 1, 0])
    position = 0
    for x in range(size_x):
        arrived = jnp.zeros((ext_z, slots), jnp.float32)
        for o in range(6):
            arrived = jnp.where(lane == letter + o, float(2**o), arrived)
        arrived = jnp.where(comb[0, x + 1, 1] < NEAR, arrived, 0.0)
        arrived = jnp.sum(arrived, axis=1, keepdims=True).astype(jnp.int32)
        for z in range(size_z):
            bits = arrived[z + 1, 0]
            for o in range(6):
                arrivals[position] = x * 256 + z * 16 + o
                position = position + (lax.shift_right_logical(bits, o) & 1)
    arrival_steps = lax.div(position + (ARRIVALS - 1), ARRIVALS)
    for extra in range(ARRIVALS):
        arrivals[position + extra] = 7

    @pl.when(overflow)
    def _():
        for k, (dx, dy, dz) in enumerate(COMBOS):
            for x in range(size_x):
                for c, step in enumerate((dx, dy, dz)):
                    tile = comb[c, x + 1 + dx, 1 + dy]
                    if dz:
                        tile = pltpu.roll(tile, (-dz) % ext_z, 0)
                    cand[x, k, c] = tile + step * sides[c]
                    if k == 0:
                        cand[x, len(COMBOS), c] = far_tile

    for x in range(size_x):
        force_t[x] = jnp.zeros((slots, slots), jnp.float32)
    for x in range(size_x):
        for c in range(3):
            arrival_force[x, c] = jnp.zeros((ext_z, slots), jnp.float32)

    pair_loop(items, steps_ref[0], own_t, cand, range(SHORT), force_t, slots, ext_z)

    def each_arrival(group, carry):
        work = []
        for g in range(ARRIVALS):
            code = arrivals[group * ARRIVALS + g]
            x = lax.shift_right_logical(code, 8)
            z = lax.shift_right_logical(code, 4) & 15
            slot = letter + (code & 15)
            pick = jnp.full((ext_z, slots), slot & (slots - 1), jnp.int32)
            own = []
            for c in range(3):
                row = comb[c, x + 1, 1, pl.ds(z + 1, 1), :]
                own.append(take(jnp.broadcast_to(row, (ext_z, slots)), pick))
            away = sub - (z + 1)
            rise = away.astype(jnp.float32) * sides[2]
            beside = jnp.abs(away) <= 1
            other = []
            for dx in (-1, 0, 1):
                for dy in (-1, 0, 1):
                    tiles = [comb[c, x + 1 + dx, 1 + dy] for c in range(3)]
                    tiles[0] = jnp.where(beside, tiles[0], FAR)
                    tiles[0] = tiles[0] + dx * sides[0] if dx else tiles[0]
                    tiles[1] = tiles[1] + dy * sides[1] if dy else tiles[1]
                    tiles[2] = tiles[2] + rise
                    other.append(tiles)
            found = row_sums(pair_force(own, other))
            found = [jnp.sum(f, axis=0, keepdims=True) for f in found]
            work.append((x, (sub == z + 1) & (lane == slot), found))
        for x, spot, found in work:
            for c in range(3):
                arrival_force[x, c] = jnp.where(spot, found[c], arrival_force[x, c])
        return carry

    lax.fori_loop(0, arrival_steps, each_arrival, 0)

    @pl.when(overflow | longest)
    def _():
        def each_x(x, x_position):
            def each_z(z, z_position):
                blocks = lax.shift_right_logical(count_ref[x, 0, z] + 7, 3)

                def each_part(part, part_position):
                    def each_block(block, position):
                        more_items[position] = part * (SHORT * 4096) + x * 256 + z * 16 + block
                        return position + 1

                    return lax.fori_loop(0, blocks, each_block, part_position)

                parts = lax.div(chunk_count[x, z] + (SHORT - 1), SHORT)
                return lax.fori_loop(1, parts, each_part, z_position)

            return lax.fori_loop(0, size_z, each_z, x_position)

        position = lax.fori_loop(0, size_x, each_x, 0)
        for more in range(GROUP):
            more_items[position + more] = slots // 8 - 1
        steps = lax.div(position + (GROUP - 1), GROUP)
        pair_loop(more_items, steps, own_t, cand, range(SHORT), force_t, slots, ext_z)

    kept = jnp.where(overflow, 0.0, 1.0)
    speed = jnp.full((ext_z, slots), letter - 1, jnp.int32)
    for x in range(size_x):
        turned = (own_t[x] * kept + force_t[x]).T * 48.0
        count = counts[x]
        base = comb[0, x + 1, 1]
        filled = count
        index = lane
        for o in range(6):
            valid = take(base, jnp.full((ext_z, slots), letter + o, jnp.int32)) < NEAR
            index = jnp.where(valid & (lane == filled), letter + o, index)
            filled = filled + jnp.where(valid, 1, 0)
        placed = take(base, index)
        alive = (lane < filled) & (placed < NEAR)
        for c in range(3):
            half = half_ref[c, x]
            blank = jnp.zeros((1, slots), jnp.float32)
            half = jnp.concatenate([blank, half, blank], axis=0)
            tile = own_ref[c, x + 1]
            sent = [
                own_ref[c, x],
                own_ref[c, x + 2],
                low_ref[c, x + 1],
                high_ref[c, x + 1],
                pltpu.roll(tile, 1, 0),
                pltpu.roll(tile, ext_z - 1, 0),
            ]
            for o in range(6):
                half = jnp.where(lane == letter + o, take(sent[o], speed), half)
            where_to = placed if c == 0 else take(comb[c, x + 1, 1], index)
            start = 3 * PART + c * ext_z
            force = turned[start : start + ext_z]
            force = jnp.where(lane >= letter, arrival_force[x, c] * 48.0, force)
            force = jnp.where(alive, take(force, index), 0.0)
            half = take(half, index) + 0.5 * step_size * force
            where_to = jnp.where(alive, where_to, 0.0)
            half = jnp.where(alive, half, 0.0)
            for z in range(size_z):
                out_place_ref[c, x, z] = where_to[z + 1 : z + 2]
                out_velocity_ref[c, x, z] = half[z + 1 : z + 2]
                out_force_ref[c, x, z] = force[z + 1 : z + 2]


def shifted(value, axis, steps):
    count = lax.axis_size(axis)
    return lax.ppermute(value, axis, [(i, (i + steps) % count) for i in range(count)])


def per_device(places, velocity, forces_old, counts, mig_atom, mig_face):
    size_x, size_y, size_z, slots = places.shape[1:]
    assert size_y == 1 and size_z == 6 and slots == 128 and size_x >= 2
    flat = (size_x, size_z, slots)
    swapped = [jnp.transpose(a, (0, 1, 3, 2, 4)) for a in (places, velocity, forces_old)]
    vmem = pl.BlockSpec(memory_space=pltpu.VMEM)
    smem = pl.BlockSpec(memory_space=pltpu.SMEM)
    slab, first, last, half = pl.pallas_call(
        pack_kernel,
        out_shape=[
            jax.ShapeDtypeStruct((4,) + flat, jnp.float32),
            jax.ShapeDtypeStruct((4, size_x, 1, slots), jnp.float32),
            jax.ShapeDtypeStruct((4, size_x, 1, slots), jnp.float32),
            jax.ShapeDtypeStruct((3,) + flat, jnp.float32),
        ],
        in_specs=[smem] * 3 + [vmem] * 3,
        out_specs=[vmem] * 4,
    )(counts, mig_atom.reshape(-1), mig_face.reshape(-1), *swapped)

    from_low = shifted(last, "gz", 1)
    from_high = shifted(first, "gz", -1)
    slab = jnp.concatenate([from_low, slab, from_high], axis=2)
    if lax.axis_size("gx") == 2:
        both = shifted(jnp.concatenate([slab[:, :1], slab[:, size_x - 1 :]], axis=1), "gx", 1)
        from_low, from_high = both[:, 1:], both[:, :1]
    else:
        from_low = shifted(slab[:, size_x - 1 :], "gx", 1)
        from_high = shifted(slab[:, :1], "gx", -1)
    slab = jnp.concatenate([from_low, slab, from_high], axis=1)
    own, letters = slab[:3], slab[3]
    low = shifted(own, "gy", 1)
    high = shifted(own, "gy", -1)
    far_low = shifted(letters, "gy", 2)
    far_high = far_low if lax.axis_size("gy") == 4 else shifted(letters, "gy", -2)

    ext_x, ext_z = size_x + 2, size_z + 2
    room = size_x * size_z * (slots // 8) + GROUP
    tile = (ext_z, slots)
    params = pltpu.CompilerParams(vmem_limit_bytes=24 * 1024 * 1024)
    own_t, begun, filled, box, excess, items, steps = pl.pallas_call(
        plane_kernel,
        out_shape=[
            jax.ShapeDtypeStruct((size_x, slots, slots), jnp.float32),
            jax.ShapeDtypeStruct((size_x, PLANE_CHUNKS - 1, 3) + tile, jnp.float32),
            jax.ShapeDtypeStruct((size_x,) + tile, jnp.int32),
            jax.ShapeDtypeStruct((6,) + tile, jnp.float32),
            jax.ShapeDtypeStruct(tile, jnp.int32),
            jax.ShapeDtypeStruct((room,), jnp.int32),
            jax.ShapeDtypeStruct((1,), jnp.int32),
        ],
        in_specs=[smem, vmem],
        out_specs=[vmem] * 5 + [smem] * 2,
        scratch_shapes=[
            pltpu.VMEM((3, 3, ext_x) + tile, jnp.float32),
            pltpu.VMEM((size_x, 1, 3) + tile, jnp.float32),
        ],
        compiler_params=params,
    )(counts, own)
    outs = pl.pallas_call(
        force_kernel,
        out_shape=[jax.ShapeDtypeStruct(swapped[0].shape, jnp.float32)] * 3,
        in_specs=[smem] * 3 + [vmem] * 11,
        out_specs=[vmem] * 3,
        scratch_shapes=[
            pltpu.VMEM((3, ext_x, 3) + tile, jnp.float32),
            pltpu.VMEM((3, 3, ext_x, 2) + tile, jnp.float32),
            pltpu.VMEM((size_x, len(COMBOS) + 1, 3) + tile, jnp.float32),
            pltpu.VMEM((size_x, slots, slots), jnp.float32),
            pltpu.VMEM((size_x, 3) + tile, jnp.float32),
            pltpu.SMEM((size_x, size_z), jnp.int32),
            pltpu.SMEM((size_x * size_z * 6 + ARRIVALS,), jnp.int32),
            pltpu.SMEM((-(-len(COMBOS) // SHORT) * (room - GROUP) + GROUP,), jnp.int32),
        ],
        compiler_params=params,
    )(counts, items, steps, own, low, high, far_low, far_high, half, own_t, begun, filled, box, excess)
    return tuple(jnp.transpose(o, (0, 1, 3, 2, 4)) for o in outs)


def solution(mesh):
    block = P(None, "gx", "gy", "gz", None)
    return jax.shard_map(
        per_device,
        mesh=mesh,
        in_specs=(
            block,
            block,
            block,
            P("gx", "gy", "gz"),
            P("gx", "gy", "gz", None),
            P("gx", "gy", "gz", None),
        ),
        out_specs=(block, block, block),
        check_vma=False,
    )
```

```python
import functools

import jax
import jax.numpy as jnp
from jax import lax
from jax.experimental import pallas as pl
from jax.experimental.pallas import tpu as pltpu
from jax.sharding import PartitionSpec as P

step_size = 0.005
cut_radius = 2.5
spacing = 1.1
edge_force = 24.0 * (2.0 * cut_radius ** (-13) - cut_radius ** (-7))

FAR = 24.0
NEAR = 16.0
MARGIN = 1.0e-3
GROUP = 48
ARRIVALS = 8
SHORT = 2
CHUNKS = 6
PLANE_CHUNKS = 3
PART = 32
APART = 0.25
COMBOS = [(dx, dy, dz) for dx in (-1, 0, 1) for dy in (-1, 0, 1) for dz in (-1, 0, 1)]


def by_weight(combos):
    return sorted(combos, key=lambda c: abs(c[0]) + abs(c[1]) + 2 * abs(c[2]))


PLANE = by_weight(c for c in COMBOS if c[1] == 0 and c != (0, 0, 0))
SIDES = by_weight(c for c in COMBOS if c[1] != 0)


def cell_sides(slot_count):
    return (4.0 * spacing, 4.0 * spacing, spacing * (slot_count // 16))


def take(tile, index):
    return jnp.take_along_axis(tile, index, axis=1, mode="promise_in_bounds")


def rows_of(ref, c, x, size_z, slots):
    sub = lax.broadcasted_iota(jnp.int32, (size_z, slots), 0)
    tile = jnp.broadcast_to(ref[c, x, 0], (size_z, slots))
    for z in range(1, size_z):
        tile = jnp.where(sub == z, ref[c, x, z], tile)
    return tile


def pack_kernel(
    count_ref, atom_ref, face_ref, place_ref, velocity_ref, force_ref,
    slab_ref, first_ref, last_ref, sides_ref, half_ref,
):
    _, size_x, size_z, _, slots = place_ref.shape
    sides = cell_sides(slots)
    sub = lax.broadcasted_iota(jnp.int32, (size_z, slots), 0)
    lane = lax.broadcasted_iota(jnp.int32, (size_z, slots), 1)
    letter = slots - 6
    entries = atom_ref.shape[0]
    atoms = [atom_ref[e] for e in range(entries)]
    faces = [face_ref[e] for e in range(entries)]
    for x in range(size_x):
        count = jnp.zeros((size_z, slots), jnp.int32)
        for z in range(size_z):
            count = jnp.where(sub == z, count_ref[x, 0, z], count)
        first_atom = (x * size_z + sub) * slots
        leaving = jnp.full((size_z, slots), -1, jnp.int32)
        face = jnp.full((size_z, slots), -8, jnp.int32)
        for e in range(entries):
            offset = atoms[e] - first_atom
            here = (offset >= 0) & (offset < slots)
            leaving = jnp.where(here, offset, leaving)
            face = jnp.where(here, faces[e], face)
        any_leaves = leaving >= 0
        picked = jnp.maximum(leaving, 0)
        order = jnp.bitwise_xor(face, 1)
        axis_of = lax.shift_right_arithmetic(face, 1)
        sign = (2 * (face & 1) - 1).astype(jnp.float32)
        alive = (lane < count) & (lane != leaving)
        letter_lane = any_leaves & (lane == letter + order)
        speed_lane = lane == letter - 1
        letters = jnp.full((size_z, slots), FAR, jnp.float32)
        for c in range(3):
            half = rows_of(velocity_ref, c, x, size_z, slots) + (
                0.5 * step_size * rows_of(force_ref, c, x, size_z, slots)
            )
            drifted = rows_of(place_ref, c, x, size_z, slots) + step_size * half
            half_ref[c, x] = half
            moved = take(drifted, picked) - jnp.where(axis_of == c, sign * sides[c], 0.0)
            tile = jnp.where(alive, drifted, FAR)
            tile = jnp.where(letter_lane, moved, tile)
            tile = jnp.where(speed_lane, take(half, picked), tile)
            slab_ref[c, x] = tile
            first_ref[c, x] = tile[:1]
            last_ref[c, x] = tile[size_z - 1 :]
            if x in (0, size_x - 1):
                sides_ref[c, min(x, 1)] = tile
            letters = jnp.where(any_leaves & (lane == letter + order - 8 * c), moved, letters)
        slab_ref[3, x] = letters
        first_ref[3, x] = letters[:1]
        last_ref[3, x] = letters[size_z - 1 :]
        if x in (0, size_x - 1):
            sides_ref[3, min(x, 1)] = letters


def append_batch(batch, scanned, chunks, filled):
    rows, slots = filled.shape
    lane = lax.broadcasted_iota(jnp.int32, (rows, slots), 1)
    rank = (lane - filled) & (slots - 1)
    packed, start = scanned[0]
    place_shift = jnp.zeros((rows, slots), jnp.int32)
    local = rank
    picks = []
    for s in range(1, len(batch)):
        packed = packed | lax.shift_left(scanned[s][0], 8 * s)
        later = rank >= start
        picks.append(later)
        place_shift = jnp.where(later, 8 * s, place_shift)
        local = jnp.where(later, rank - start, local)
        start = start + scanned[s][1]
    position = jnp.zeros((rows, slots), jnp.int32)
    step = slots // 2
    while step >= 1:
        probe = take(packed, position + (step - 1))
        probe = lax.shift_right_logical(probe, place_shift) & 255
        position = jnp.where(probe <= local, position + step, position)
        step //= 2
    moved = []
    for c in range(3):
        value = take(batch[0][c], position)
        for s in range(1, len(batch)):
            value = jnp.where(picks[s - 1], take(batch[s][c], position), value)
        moved.append(value)
    chunk_id = lax.shift_right_logical(filled + rank, slots.bit_length() - 1)
    chunk_id = jnp.where(rank < start, chunk_id, -1)
    for k in range(len(chunks)):
        chosen = chunk_id == k
        chunks[k] = [jnp.where(chosen, moved[c], chunks[k][c]) for c in range(3)]
    return chunks, filled + start, start


def pair_force(own, other):
    total = [None, None, None]
    for row in other:
        delta = [own[c] - row[c] for c in range(3)]
        square = delta[0] * delta[0] + delta[1] * delta[1] + delta[2] * delta[2]
        square = jnp.minimum(jnp.maximum(square, APART), cut_radius * cut_radius)
        root = lax.rsqrt(square)
        inverse = root * root
        fourth = inverse * inverse
        sixth = fourth * inverse
        strength = (sixth - 0.5) * (fourth * fourth) - (edge_force / 48.0) * root
        for c in range(3):
            part = delta[c] * strength
            total[c] = part if total[c] is None else total[c] + part
    return total


def row_sums(found):
    return [jnp.sum(f, axis=1, keepdims=True) for f in found]


def scan_weights(slots):
    row_id = lax.broadcasted_iota(jnp.int32, (slots, 2 * slots), 0)
    col_id = lax.broadcasted_iota(jnp.int32, (slots, 2 * slots), 1)
    return jnp.where(row_id <= col_id, 1.0, 0.0).astype(jnp.bfloat16)


def append_sources(sources, chunks, filled, excess, weights):
    slots = weights.shape[0]
    rows = filled.shape[0]
    masks = jnp.concatenate([jnp.where(m, 1.0, 0.0) for m, _ in sources], axis=0)
    scanned = jnp.dot(
        masks.astype(jnp.bfloat16), weights, preferred_element_type=jnp.float32
    ).astype(jnp.int32)
    split = []
    for s in range(len(sources)):
        part = scanned[rows * s : rows * (s + 1)]
        split.append((part[:, :slots], part[:, slots:]))
    batches = -(-len(sources) // 4)
    for batch in range(batches):
        ids = range(batch, len(sources), batches)
        chunks, filled, added = append_batch(
            [sources[s][1] for s in ids], [split[s] for s in ids], chunks, filled
        )
        excess = jnp.maximum(excess, added - slots)
    return chunks, filled, jnp.maximum(excess, filled - len(chunks) * slots)


def sideways(tiles, dx, side, lower, upper):
    real = tiles[0] < NEAR
    if dx:
        tiles = [tiles[0] + dx * side] + tiles[1:]
        real = real & ((tiles[0] > lower) if dx < 0 else (tiles[0] < upper))
    return real, tiles


def pair_loop(items, steps, own_ref, cand, chunk_ids, sums_ref, adding):
    slots = own_ref.shape[2]
    lane = lax.broadcasted_iota(jnp.int32, (8, slots), 1)
    shift = slots.bit_length() - 1
    row_id = lax.broadcasted_iota(jnp.int32, (slots, 3 * slots), 0)
    col_id = lax.broadcasted_iota(jnp.int32, (slots, 3 * slots), 1)
    of_axis = lax.shift_right_logical(row_id & (PART - 1), 3)
    spread = (of_axis == lax.shift_right_logical(col_id, shift)) & (row_id < 3 * PART)
    spread = jnp.where(spread, 1.0, 0.0).astype(jnp.bfloat16)
    row_id = lax.broadcasted_iota(jnp.int32, (3 * slots, slots), 0)
    col_id = lax.broadcasted_iota(jnp.int32, (3 * slots, slots), 1) - 3 * PART
    summing = (lax.shift_right_arithmetic(col_id, 3) == lax.shift_right_logical(row_id, shift))
    summing = jnp.where(summing, 1.0, 0.0).astype(jnp.bfloat16)
    summing = jnp.concatenate([summing, summing], axis=0)

    def item(group, g):
        code = items[group * GROUP + g]
        x = lax.shift_right_logical(code, 8) & 15
        z = lax.shift_right_logical(code, 4) & 15
        rows = pl.ds(pl.multiple_of((code & 15) * 8, 8), 8)
        return x, z, lax.shift_right_logical(code, 12), rows

    def spread_columns(group):
        held = []
        for g in range(GROUP):
            x, z, _, rows = item(group, g)
            held.append(jnp.where((lane & 7) == z + 1, own_ref[x, rows, :], 0.0))
        return jnp.dot(
            jnp.concatenate(held, axis=0).astype(jnp.bfloat16),
            spread,
            preferred_element_type=jnp.float32,
        )

    def add_rows(group, sums):
        for g in range(GROUP):
            x, z, _, rows = item(group, g)
            value = sums[8 * g : 8 * g + 8]
            sums_ref[x, z, rows, :] = sums_ref[x, z, rows, :] + value if adding else value

    def each_group(group, carry):
        columns = spread_columns(group)
        found = []
        for g in range(GROUP):
            x, z, first, _ = item(group, g)
            own = [columns[8 * g : 8 * g + 8, c * slots : (c + 1) * slots] for c in range(3)]
            other = [
                [cand[x, first + k, c, pl.ds(z + 1, 1), :] for c in range(3)] for k in chunk_ids
            ]
            found.append(pair_force(own, other))
        found = [jnp.concatenate([f[c] for f in found], axis=0) for c in range(3)]
        rounded = [f.astype(jnp.bfloat16) for f in found]
        rest = [(f - r.astype(jnp.float32)).astype(jnp.bfloat16) for f, r in zip(found, rounded)]
        sums = jnp.dot(
            jnp.concatenate(rounded + rest, axis=1), summing, preferred_element_type=jnp.float32
        )
        add_rows(group, sums)
        return carry

    lax.fori_loop(0, steps, each_group, 0)


def joined_sums(sums_ref, x):
    _, size_z, slots, _ = sums_ref.shape
    lane = lax.broadcasted_iota(jnp.int32, (slots, slots), 1)
    value = jnp.zeros((slots, slots), jnp.float32)
    for z in range(size_z):
        value = jnp.where((lane & 7) == z + 1, sums_ref[x, z], value)
    return jnp.where(lane >= 3 * PART, value, 0.0)


def own_kernel(count_ref, slab_ref, own_t, box_ref, items, steps_ref):
    _, size_x, size_z, slots = slab_ref.shape
    ext_z = size_z + 2
    lane = lax.broadcasted_iota(jnp.int32, (size_z, slots), 1)
    stayed = lane < slots - 7

    position = 0
    for x in range(size_x):
        for z in range(size_z):
            code = x * 256 + z * 16
            for block in range(slots // 8):
                items[position + block] = code + block
            position = position + lax.shift_right_logical(count_ref[x, 0, z] + 7, 3)
    steps_ref[0] = lax.div(position + (GROUP - 1), GROUP)
    for extra in range(GROUP):
        items[position + extra] = slots // 8 - 1

    for c in range(3):
        low_tile = jnp.full((size_z, slots), FAR, jnp.float32)
        high_tile = jnp.full((size_z, slots), -FAR, jnp.float32)
        for x in range(size_x):
            tile = slab_ref[c, x]
            real = stayed & (tile < NEAR)
            low_tile = jnp.minimum(low_tile, jnp.where(real, tile, FAR))
            high_tile = jnp.maximum(high_tile, jnp.where(real, tile, -FAR))
        low = jnp.min(low_tile, axis=(0, 1), keepdims=True) - (cut_radius + MARGIN)
        high = jnp.max(high_tile, axis=(0, 1), keepdims=True) + (cut_radius + MARGIN)
        box_ref[c] = jnp.broadcast_to(low, (ext_z, slots))
        box_ref[3 + c] = jnp.broadcast_to(high, (ext_z, slots))

    blank = jnp.full((1, slots), FAR, jnp.float32)
    for x in range(size_x):
        split = []
        rest = [
            jnp.concatenate([blank, jnp.where(stayed, slab_ref[c, x], FAR), blank], axis=0)
            for c in range(3)
        ]
        for _ in range(3):
            rounded = [r.astype(jnp.bfloat16).astype(jnp.float32) for r in rest]
            rest = [r - h for r, h in zip(rest, rounded)]
            split += rounded + [jnp.zeros((PART - 3 * ext_z, slots), jnp.float32)]
        split.append(jnp.zeros((slots - 3 * PART, slots), jnp.float32))
        own_t[x] = jnp.concatenate(split, axis=0).T


def plane_kernel(
    count_ref, items, steps_ref, own_ref, own_t, box_ref,
    begun_force, begun, filled_ref, excess_ref,
    reach, cand, sums,
):
    _, ext_x, ext_z, slots = own_ref.shape
    size_x, size_z = ext_x - 2, ext_z - 2
    sides = cell_sides(slots)
    letter = slots - 6
    sub = lax.broadcasted_iota(jnp.int32, (ext_z, slots), 0)
    lane = lax.broadcasted_iota(jnp.int32, (ext_z, slots), 1)
    inner = (sub >= 1) & (sub <= size_z)
    stayed = lane < letter - 1
    far_tile = jnp.full((ext_z, slots), FAR, jnp.float32)

    lower = [box_ref[c] for c in range(3)]
    upper = [box_ref[3 + c] for c in range(3)]

    centers = {}
    from_z_low = (lane == letter + 4) & (sub > 0)
    from_z_high = (lane == letter + 5) & (sub < ext_z - 1)
    for x in range(ext_x):
        settled = []
        for c in range(3):
            tile = own_ref[c, x]
            out = jnp.where(stayed, tile, FAR)
            if x > 0:
                out = jnp.where(lane == letter, own_ref[c, x - 1], out)
            if x < ext_x - 1:
                out = jnp.where(lane == letter + 1, own_ref[c, x + 1], out)
            out = jnp.where(from_z_low, pltpu.roll(tile, 1, 0), out)
            settled.append(jnp.where(from_z_high, pltpu.roll(tile, ext_z - 1, 0), out))
        centers[x] = settled
        for dz in (-1, 0, 1):
            tiles = settled
            usable = inner
            if dz:
                tiles = [pltpu.roll(t, (-dz) % ext_z, 0) for t in tiles]
                tiles[2] = tiles[2] + dz * sides[2]
                usable = usable & ((tiles[2] > lower[2]) if dz < 0 else (tiles[2] < upper[2]))
            reach[dz + 1, 0, x] = jnp.where(usable, tiles[0], FAR)
            reach[dz + 1, 1, x] = tiles[1]
            reach[dz + 1, 2, x] = tiles[2]

    weights = scan_weights(slots)
    excess = jnp.full((ext_z, slots), -1, jnp.int32)
    for x in range(size_x):
        count = jnp.zeros((ext_z, slots), jnp.int32)
        for z in range(size_z):
            count = jnp.where(sub == z + 1, count_ref[x, 0, z], count)
        center = centers[x + 1]
        sources = [(inner & (lane >= letter) & (center[0] < NEAR), center)]
        for dx, _, dz in PLANE:
            tiles = [reach[dz + 1, c, x + 1 + dx] for c in range(3)]
            sources.append(sideways(tiles, dx, sides[0], lower[0], upper[0]))
        chunks = [[jnp.where(lane < count, t, FAR) for t in center]]
        chunks += [[far_tile] * 3 for _ in range(PLANE_CHUNKS - 1)]
        chunks, filled, excess = append_sources(sources, chunks, count, excess, weights)
        filled_ref[x] = jnp.maximum(filled - slots, 0)
        for c in range(3):
            cand[x, 0, c] = chunks[0][c]
            for k in range(PLANE_CHUNKS - 1):
                begun[x, k, c] = chunks[k + 1][c]
    excess_ref[...] = excess
    pair_loop(items, steps_ref[0], own_t, cand, (0,), sums, False)
    for x in range(size_x):
        begun_force[x] = joined_sums(sums, x)


def force_kernel(
    count_ref,
    items,
    steps_ref,
    own_ref,
    low_ref,
    high_ref,
    far_low_ref,
    far_high_ref,
    half_ref,
    own_t,
    box_ref,
    begun_force,
    begun,
    filled_ref,
    excess_ref,
    out_place_ref,
    out_velocity_ref,
    out_force_ref,
    comb,
    reach,
    cand,
    sums,
    arrival_force,
    chunk_count,
    arrivals,
    more_items,
):
    _, ext_x, ext_z, slots = own_ref.shape
    size_x, size_z = ext_x - 2, ext_z - 2
    sides = cell_sides(slots)
    letter = slots - 6
    sub = lax.broadcasted_iota(jnp.int32, (ext_z, slots), 0)
    lane = lax.broadcasted_iota(jnp.int32, (ext_z, slots), 1)
    inner = (sub >= 1) & (sub <= size_z)
    far_tile = jnp.full((ext_z, slots), FAR, jnp.float32)
    planes = [low_ref, own_ref, high_ref]
    lower = [box_ref[c] for c in range(3)]
    upper = [box_ref[3 + c] for c in range(3)]

    from_z_low = (lane == letter + 4) & (sub > 0)
    from_z_high = (lane == letter + 5) & (sub < ext_z - 1)
    for x in range(ext_x):
        for y in range(3):
            for c in range(3):
                tile = planes[y][c, x]
                out = jnp.where(lane < letter - 1, tile, FAR)
                if x > 0:
                    out = jnp.where(lane == letter, planes[y][c, x - 1], out)
                if x < ext_x - 1:
                    out = jnp.where(lane == letter + 1, planes[y][c, x + 1], out)
                below = planes[y - 1][c, x] if y > 0 else pltpu.roll(far_low_ref[x], 8 * c, 1)
                above = planes[y + 1][c, x] if y < 2 else pltpu.roll(far_high_ref[x], 8 * c, 1)
                out = jnp.where(lane == letter + 2, below, out)
                out = jnp.where(lane == letter + 3, above, out)
                out = jnp.where(from_z_low, pltpu.roll(tile, 1, 0), out)
                out = jnp.where(from_z_high, pltpu.roll(tile, ext_z - 1, 0), out)
                comb[c, x, y] = out

    spare = lane == letter - 2
    for x in range(ext_x):
        for side, y in enumerate((0, 2)):
            crossed = [
                pltpu.roll(planes[y][c, x], slots - 4 - side, 1) for c in range(3)
            ]
            settled = [comb[c, x, y] for c in range(3)]
            settled[1] = settled[1] + (y - 1) * sides[1]
            settled = [jnp.where(spare, a, b) for a, b in zip(crossed, settled)]
            reached = (settled[1] > lower[1]) if y == 0 else (settled[1] < upper[1])
            settled[0] = jnp.where(reached, settled[0], FAR)
            for dz in (-1, 0, 1):
                tiles = settled
                usable = inner
                if dz:
                    tiles = [pltpu.roll(t, (-dz) % ext_z, 0) for t in tiles]
                    tiles[2] = tiles[2] + dz * sides[2]
                    usable = usable & ((tiles[2] > lower[2]) if dz < 0 else (tiles[2] < upper[2]))
                reach[dz + 1, 0, x, side] = jnp.where(usable, tiles[0], FAR)
                reach[dz + 1, 1, x, side] = tiles[1]
                reach[dz + 1, 2, x, side] = tiles[2]

    weights = scan_weights(slots)
    excess = excess_ref[...]
    counts = []
    for x in range(size_x):
        count = jnp.zeros((ext_z, slots), jnp.int32)
        for z in range(size_z):
            count = jnp.where(sub == z + 1, count_ref[x, 0, z], count)
        counts.append(count)

    chunk_tiles = []
    for x in range(size_x):
        sources = []
        for dx, dy, dz in SIDES:
            tiles = [reach[dz + 1, c, x + 1 + dx, (dy + 1) // 2] for c in range(3)]
            sources.append(sideways(tiles, dx, sides[0], lower[0], upper[0]))
        chunks = [[begun[x, k, c] for c in range(3)] for k in range(PLANE_CHUNKS - 1)]
        chunks += [[far_tile] * 3 for _ in range(CHUNKS - PLANE_CHUNKS + 1)]
        chunks, filled, excess = append_sources(sources, chunks, filled_ref[x], excess, weights)
        for k in range(CHUNKS):
            for c in range(3):
                cand[x, k, c] = chunks[k][c]
        chunk_tiles.append(lax.shift_right_logical(filled + (slots - 1), slots.bit_length() - 1))

    overflow = jnp.max(excess.astype(jnp.float32)) > 0.0
    longest = functools.reduce(jnp.maximum, chunk_tiles)
    longest = jnp.max(jnp.where(inner, longest, 0).astype(jnp.float32)) > SHORT
    for x in range(size_x):
        for z in range(size_z):
            chunk_count[x, z] = jnp.where(overflow, len(COMBOS), chunk_tiles[x][z + 1, 0])
    position = 0
    for x in range(size_x):
        arrived = jnp.zeros((ext_z, slots), jnp.float32)
        for o in range(6):
            arrived = jnp.where(lane == letter + o, float(2**o), arrived)
        arrived = jnp.where(comb[0, x + 1, 1] < NEAR, arrived, 0.0)
        arrived = jnp.sum(arrived, axis=1, keepdims=True).astype(jnp.int32)
        for z in range(size_z):
            bits = arrived[z + 1, 0]
            for o in range(6):
                arrivals[position] = x * 256 + z * 16 + o
                position = position + (lax.shift_right_logical(bits, o) & 1)
    arrival_steps = lax.div(position + (ARRIVALS - 1), ARRIVALS)
    for extra in range(ARRIVALS):
        arrivals[position + extra] = 7

    @pl.when(overflow)
    def _():
        for k, (dx, dy, dz) in enumerate(COMBOS):
            for x in range(size_x):
                for c, step in enumerate((dx, dy, dz)):
                    tile = comb[c, x + 1 + dx, 1 + dy]
                    if dz:
                        tile = pltpu.roll(tile, (-dz) % ext_z, 0)
                    cand[x, k, c] = tile + step * sides[c]
                    if k == 0:
                        cand[x, len(COMBOS), c] = far_tile

    for x in range(size_x):
        for c in range(3):
            arrival_force[x, c] = jnp.zeros((ext_z, slots), jnp.float32)

    pair_loop(items, steps_ref[0], own_t, cand, range(SHORT), sums, False)

    def each_arrival(group, carry):
        work = []
        for g in range(ARRIVALS):
            code = arrivals[group * ARRIVALS + g]
            x = lax.shift_right_logical(code, 8)
            z = lax.shift_right_logical(code, 4) & 15
            slot = letter + (code & 15)
            pick = jnp.full((ext_z, slots), slot & (slots - 1), jnp.int32)
            own = []
            for c in range(3):
                row = comb[c, x + 1, 1, pl.ds(z + 1, 1), :]
                own.append(take(jnp.broadcast_to(row, (ext_z, slots)), pick))
            away = sub - (z + 1)
            rise = away.astype(jnp.float32) * sides[2]
            beside = jnp.abs(away) <= 1
            other = []
            for dx in (-1, 0, 1):
                for dy in (-1, 0, 1):
                    tiles = [comb[c, x + 1 + dx, 1 + dy] for c in range(3)]
                    tiles[0] = jnp.where(beside, tiles[0], FAR)
                    tiles[0] = tiles[0] + dx * sides[0] if dx else tiles[0]
                    tiles[1] = tiles[1] + dy * sides[1] if dy else tiles[1]
                    tiles[2] = tiles[2] + rise
                    other.append(tiles)
            found = row_sums(pair_force(own, other))
            found = [jnp.sum(f, axis=0, keepdims=True) for f in found]
            work.append((x, (sub == z + 1) & (lane == slot), found))
        for x, spot, found in work:
            for c in range(3):
                arrival_force[x, c] = jnp.where(spot, found[c], arrival_force[x, c])
        return carry

    lax.fori_loop(0, arrival_steps, each_arrival, 0)

    @pl.when(overflow | longest)
    def _():
        def each_x(x, x_position):
            def each_z(z, z_position):
                blocks = lax.shift_right_logical(count_ref[x, 0, z] + 7, 3)

                def each_part(part, part_position):
                    def each_block(block, position):
                        more_items[position] = part * (SHORT * 4096) + x * 256 + z * 16 + block
                        return position + 1

                    return lax.fori_loop(0, blocks, each_block, part_position)

                parts = lax.div(chunk_count[x, z] + (SHORT - 1), SHORT)
                return lax.fori_loop(1, parts, each_part, z_position)

            return lax.fori_loop(0, size_z, each_z, x_position)

        position = lax.fori_loop(0, size_x, each_x, 0)
        for more in range(GROUP):
            more_items[position + more] = slots // 8 - 1
        steps = lax.div(position + (GROUP - 1), GROUP)
        pair_loop(
            more_items, steps, own_t, cand, range(SHORT), sums, True
        )

    kept = jnp.where(overflow, 0.0, 1.0)
    speed = jnp.full((ext_z, slots), letter - 1, jnp.int32)
    for x in range(size_x):
        turned = (begun_force[x] * kept + joined_sums(sums, x)).T * 48.0
        count = counts[x]
        base = comb[0, x + 1, 1]
        filled = count
        index = lane
        for o in range(6):
            valid = take(base, jnp.full((ext_z, slots), letter + o, jnp.int32)) < NEAR
            index = jnp.where(valid & (lane == filled), letter + o, index)
            filled = filled + jnp.where(valid, 1, 0)
        placed = take(base, index)
        alive = (lane < filled) & (placed < NEAR)
        for c in range(3):
            half = half_ref[c, x]
            blank = jnp.zeros((1, slots), jnp.float32)
            half = jnp.concatenate([blank, half, blank], axis=0)
            tile = own_ref[c, x + 1]
            sent = [
                own_ref[c, x],
                own_ref[c, x + 2],
                low_ref[c, x + 1],
                high_ref[c, x + 1],
                pltpu.roll(tile, 1, 0),
                pltpu.roll(tile, ext_z - 1, 0),
            ]
            for o in range(6):
                half = jnp.where(lane == letter + o, take(sent[o], speed), half)
            where_to = placed if c == 0 else take(comb[c, x + 1, 1], index)
            start = 3 * PART + c * ext_z
            force = turned[start : start + ext_z]
            force = jnp.where(lane >= letter, arrival_force[x, c] * 48.0, force)
            force = jnp.where(alive, take(force, index), 0.0)
            half = take(half, index) + 0.5 * step_size * force
            where_to = jnp.where(alive, where_to, 0.0)
            half = jnp.where(alive, half, 0.0)
            for z in range(size_z):
                out_place_ref[c, x, z] = where_to[z + 1 : z + 2]
                out_velocity_ref[c, x, z] = half[z + 1 : z + 2]
                out_force_ref[c, x, z] = force[z + 1 : z + 2]


def shifted(value, axis, steps):
    count = lax.axis_size(axis)
    return lax.ppermute(value, axis, [(i, (i + steps) % count) for i in range(count)])


def per_device(places, velocity, forces_old, counts, mig_atom, mig_face):
    size_x, size_y, size_z, slots = places.shape[1:]
    assert size_y == 1 and size_z == 6 and slots == 128 and size_x >= 2
    flat = (size_x, size_z, slots)
    swapped = [jnp.transpose(a, (0, 1, 3, 2, 4)) for a in (places, velocity, forces_old)]
    vmem = pl.BlockSpec(memory_space=pltpu.VMEM)
    smem = pl.BlockSpec(memory_space=pltpu.SMEM)
    slab, first, last, faces, half = pl.pallas_call(
        pack_kernel,
        out_shape=[
            jax.ShapeDtypeStruct((4,) + flat, jnp.float32),
            jax.ShapeDtypeStruct((4, size_x, 1, slots), jnp.float32),
            jax.ShapeDtypeStruct((4, size_x, 1, slots), jnp.float32),
            jax.ShapeDtypeStruct((4, 2, size_z, slots), jnp.float32),
            jax.ShapeDtypeStruct((3,) + flat, jnp.float32),
        ],
        in_specs=[smem] * 3 + [vmem] * 3,
        out_specs=[vmem] * 5,
    )(counts, mig_atom.reshape(-1), mig_face.reshape(-1), *swapped)

    ext_x, ext_z = size_x + 2, size_z + 2
    room = size_x * size_z * (slots // 8) + GROUP
    tile = (ext_z, slots)
    params = pltpu.CompilerParams(vmem_limit_bytes=24 * 1024 * 1024)
    own_t, box, items, steps = pl.pallas_call(
        own_kernel,
        out_shape=[
            jax.ShapeDtypeStruct((size_x, slots, slots), jnp.float32),
            jax.ShapeDtypeStruct((6,) + tile, jnp.float32),
            jax.ShapeDtypeStruct((room,), jnp.int32),
            jax.ShapeDtypeStruct((1,), jnp.int32),
        ],
        in_specs=[smem, vmem],
        out_specs=[vmem] * 2 + [smem] * 2,
        compiler_params=params,
    )(counts, slab)

    from_low = shifted(last, "gz", 1)
    from_high = shifted(first, "gz", -1)
    from_low, from_high, own_t = lax.optimization_barrier((from_low, from_high, own_t))
    ends = [jnp.concatenate([f[:, :1], f[:, size_x - 1 :]], axis=1) for f in (from_low, from_high)]
    faces = jnp.concatenate([ends[0], faces, ends[1]], axis=2)
    slab = jnp.concatenate([from_low, slab, from_high], axis=2)
    if lax.axis_size("gx") == 2:
        both = shifted(faces, "gx", 1)
        from_low, from_high = both[:, 1:], both[:, :1]
    else:
        from_low = shifted(faces[:, 1:], "gx", 1)
        from_high = shifted(faces[:, :1], "gx", -1)
    slab = jnp.concatenate([from_low, slab, from_high], axis=1)
    own, letters = slab[:3], slab[3]
    low = shifted(own, "gy", 1)
    high = shifted(own, "gy", -1)
    far_low = shifted(letters, "gy", 2)
    far_high = far_low if lax.axis_size("gy") == 4 else shifted(letters, "gy", -2)

    begun_force, begun, filled, excess = pl.pallas_call(
        plane_kernel,
        out_shape=[
            jax.ShapeDtypeStruct((size_x, slots, slots), jnp.float32),
            jax.ShapeDtypeStruct((size_x, PLANE_CHUNKS - 1, 3) + tile, jnp.float32),
            jax.ShapeDtypeStruct((size_x,) + tile, jnp.int32),
            jax.ShapeDtypeStruct(tile, jnp.int32),
        ],
        in_specs=[smem] * 3 + [vmem] * 3,
        out_specs=[vmem] * 4,
        scratch_shapes=[
            pltpu.VMEM((3, 3, ext_x) + tile, jnp.float32),
            pltpu.VMEM((size_x, 1, 3) + tile, jnp.float32),
            pltpu.VMEM((size_x, size_z, slots, slots), jnp.float32),
        ],
        compiler_params=params,
    )(counts, items, steps, own, own_t, box)
    outs = pl.pallas_call(
        force_kernel,
        out_shape=[jax.ShapeDtypeStruct(swapped[0].shape, jnp.float32)] * 3,
        in_specs=[smem] * 3 + [vmem] * 12,
        out_specs=[vmem] * 3,
        scratch_shapes=[
            pltpu.VMEM((3, ext_x, 3) + tile, jnp.float32),
            pltpu.VMEM((3, 3, ext_x, 2) + tile, jnp.float32),
            pltpu.VMEM((size_x, len(COMBOS) + 1, 3) + tile, jnp.float32),
            pltpu.VMEM((size_x, size_z, slots, slots), jnp.float32),
            pltpu.VMEM((size_x, 3) + tile, jnp.float32),
            pltpu.SMEM((size_x, size_z), jnp.int32),
            pltpu.SMEM((size_x * size_z * 6 + ARRIVALS,), jnp.int32),
            pltpu.SMEM((-(-len(COMBOS) // SHORT) * (room - GROUP) + GROUP,), jnp.int32),
        ],
        compiler_params=params,
    )(counts, items, steps, own, low, high, far_low, far_high, half,
      own_t, box, begun_force, begun, filled, excess)
    return tuple(jnp.transpose(o, (0, 1, 3, 2, 4)) for o in outs)


def solution(mesh):
    block = P(None, "gx", "gy", "gz", None)
    return jax.shard_map(
        per_device,
        mesh=mesh,
        in_specs=(
            block,
            block,
            block,
            P("gx", "gy", "gz"),
            P("gx", "gy", "gz", None),
            P("gx", "gy", "gz", None),
        ),
        out_specs=(block, block, block),
        check_vma=False,
    )
```
